32 devices in a mesh: cache: 8 (over z, y), cand: 4 (over x, core).
Axes of the slice: x: 2, y: 2, z: 4, core: 2. Of those that a mesh axis runs over, the one named last changes fastest.
Arguments:
- cand_states: bfloat16 [1024, 16, 1024], P('cand', 'cache'), may hold values from -6 to 6
- in_proj: bfloat16 [1024, 4, 1024], P(None, None, 'cand'), may hold values from -0.1875 to 0.1875
- out_proj: bfloat16 [1024, 1024], P('cand'), may hold values from -0.1875 to 0.1875
- history: bfloat16 [8, 16, 2, 512, 1024], P('cache', None, None, None, 'cand'), may hold values from -6 to 6
- lengths: int32 [16], replicated, may hold values from 2048 to 4096, as said below
- rank_users: int32 [16], replicated, may hold values from 0 to 15, each once
- recency_bias: float32 [8, 14], P('cand'), may hold values from -4 to 4
- score_weight: float32 [1024], replicated, may hold values from -0.1875 to 0.1875
Outputs:
- layer_out: bfloat16 [1024, 16, 1024], P('cand', 'cache')
- scores: float32 [1024, 16], P('cand', 'cache')
The draws below stay inside these ranges and needn't reach their ends.
Inputs may be any that keep to these rules, and one draw needn't show every extreme that they name: `lengths`: every length is a multiple of 128; some user's length is exactly 4096. `rank_users`: each user is ranked in exactly one slot.
All inputs are finite; a program needn't handle non-finite values.
Results may differ from the reference program's by a relative error of at most 0.008.
Values may be sent and summed in bfloat16 or wider, within the bound.
No kernel may reach another device: no remote copies, remote signals or barrier semaphores. Data moves between devices by JAX's collectives and lax.ppermute only.
A program may use at most 128 MiB of HBM per device.

```python
import jax
import jax.numpy as jnp
from jax import lax

D = 1024
HEADS = 8
HD = 128
BLOCK = 128
BUCKETS = 14
H_MAX = 4096
SHARDS = 8
USERS = 16
CANDS = 1024
PAGE_EV = 512


def draw_lengths(key, part):
    blocks_max = H_MAX // BLOCK
    counts = jax.random.randint(jax.random.fold_in(key, 11), (USERS,), blocks_max // 2, blocks_max + 1)
    longest = jax.random.randint(jax.random.fold_in(key, 12), (), 0, USERS)
    counts = jnp.where(jnp.arange(USERS) == longest, blocks_max, counts)
    return (counts * BLOCK).astype(jnp.int32)


def level_of(own_key, shape, cuts, least, top_value):
    factor_of, own = 1.0, jax.random.fold_in(own_key, 6)
    for dim, parts in cuts:
        steps = jnp.exp(jax.random.uniform(jax.random.fold_in(own, dim), (parts,), jnp.float32, least / len(cuts), top_value / len(cuts)))
        factor_of = factor_of * jnp.repeat(steps, shape[dim] // parts).reshape([-1 if axis == dim else 1 for axis in range(len(shape))])
    return factor_of


def scatter_about(rng, extent, scale, most, pieces=(), held_as=jnp.bfloat16):
    drawn = jax.random.normal(rng, extent, jnp.float32) * scale
    if len(pieces) > 0:
        drawn = level_of(rng, extent, pieces, -0.22, 0.18) * drawn
    return jnp.clip(drawn, min=-most, max=most).astype(held_as)


def setup_inputs(seed: int = 0) -> dict:
    key_of = jax.random.split(jax.random.key(seed), 9)
    cand_states = scatter_about(key_of[0], (CANDS, USERS, D), 1.0, 6.0, ((0, 4), (1, 8)))
    in_proj = scatter_about(key_of[1], (D, 4, D), D ** -0.5, 0.1875, ((2, 4),))
    out_proj = scatter_about(key_of[2], (D, D), D ** -0.5, 0.1875, ((0, 4),))
    history = scatter_about(key_of[3], (SHARDS, USERS, 2, PAGE_EV, D), 1.0, 6.0, ((0, 8), (4, 4)))
    lengths = draw_lengths(jax.random.fold_in(key_of[8], 71), 0)
    rank_users = jax.random.permutation(key_of[5], USERS).astype(jnp.int32)
    recency_bias = scatter_about(key_of[6], (HEADS, BUCKETS), 1.0, 4.0, ((0, 4),), jnp.float32)
    score_weight = scatter_about(key_of[7], (D,), D ** -0.5, 0.1875, (), jnp.float32)
    return {"cand_states": cand_states, "in_proj": in_proj, "out_proj": out_proj, "history": history, "lengths": lengths, "rank_users": rank_users, "recency_bias": recency_bias, "score_weight": score_weight}


EPSILON = 1e-06

def bucket_index(distance, bucket_count):
    powers = 2 ** jnp.arange(bucket_count - 1, dtype=jnp.int32)
    return lax.optimization_barrier(jnp.sum((distance[..., None] >= powers).astype(jnp.int32), axis=-1)).astype(jnp.int32)

def reference(cand_states, in_proj, out_proj, history, lengths, rank_users, recency_bias, score_weight):
    float_states = cand_states.astype(jnp.float32)
    normed = (float_states * lax.rsqrt(lax.optimization_barrier(jnp.mean(float_states * float_states, axis=-1, keepdims=True)) + EPSILON)).astype(jnp.bfloat16)
    projected = jnp.dot(normed.reshape(CANDS * USERS, D), in_proj.reshape(D, 4 * D), preferred_element_type=jnp.float32)
    projected = jax.nn.silu(projected).astype(jnp.bfloat16).reshape(CANDS, USERS, 4, D)
    scale = HD ** (-0.5)
    cache_ids = jnp.arange(SHARDS, dtype=jnp.int32)[:, None]
    event_ids = jnp.arange(PAGE_EV, dtype=jnp.int32)[None, :]

    def attend_user(slot_index):
        user = rank_users[slot_index].astype(jnp.int32)
        length = lengths[user]
        stored = lax.dynamic_index_in_dim(history, user, 1, keepdims=False)
        hist_keys = stored[:, 0].reshape(H_MAX, HEADS, HD).astype(jnp.float32)
        hist_values = stored[:, 1].reshape(H_MAX, HEADS, HD).astype(jnp.float32)
        block_ids = event_ids // BLOCK * SHARDS + jnp.remainder(cache_ids - user, SHARDS)
        positions = (block_ids * BLOCK + event_ids % BLOCK).reshape(H_MAX)
        usable = positions < length
        distance = jnp.maximum(length - positions, 0)
        bias_table = recency_bias[:, bucket_index(distance, BUCKETS)]
        own = lax.dynamic_index_in_dim(projected, slot_index, 1, keepdims=False).astype(jnp.float32)
        gates = own[:, 0].reshape(CANDS, HEADS, HD)
        own_values = own[:, 1].reshape(CANDS, HEADS, HD)
        queries = own[:, 2].reshape(CANDS, HEADS, HD)
        own_keys = own[:, 3].reshape(CANDS, HEADS, HD)
        scores = jnp.einsum('chd,khd->chk', queries, hist_keys) * scale + bias_table[None]
        weights = jnp.where(usable[None, None, :], jax.nn.silu(scores), 0.0).astype(jnp.bfloat16)
        weights = lax.optimization_barrier(weights).astype(jnp.float32)
        totals = jnp.einsum('chk,khd->chd', weights, hist_values)
        self_scores = lax.optimization_barrier(jnp.sum(queries * own_keys, axis=-1)) * scale + recency_bias[:, 0][None, :]
        totals = totals + jax.nn.silu(self_scores)[..., None] * own_values
        normalized = totals * lax.rsqrt(lax.optimization_barrier(jnp.mean(totals * totals, axis=-1, keepdims=True)) + EPSILON)
        return (normalized * gates).astype(jnp.bfloat16).reshape(CANDS, D)
    gated = lax.map(attend_user, jnp.arange(USERS, dtype=jnp.int32))
    gated = jnp.transpose(gated, (1, 0, 2))
    branch = jnp.dot(gated.reshape(CANDS * USERS, D), out_proj, preferred_element_type=jnp.float32).reshape(CANDS, USERS, D)
    layer_sum = float_states + branch
    scores_out = lax.optimization_barrier(jnp.sum(layer_sum * score_weight, axis=-1))
    return (layer_sum.astype(jnp.bfloat16), scores_out)
```

```python
import functools

import jax
import jax.numpy as jnp
from jax import lax
from jax.experimental import pallas as pl
from jax.experimental.pallas import tpu as pltpu
from jax.sharding import PartitionSpec as P

BLOCK = 128
EPSILON = 1e-06
MASKED = -1e30
VMEM = 48 * 1024 * 1024


def params():
    return pltpu.CompilerParams(vmem_limit_bytes=VMEM)


def tied(*arrays):
    return lax.optimization_barrier(arrays)


def bias_rows(recency_bias, most_blocks):
    bucket_count = recency_bias.shape[1]
    ends = jnp.arange(1, most_blocks + 1, dtype=jnp.int32)[:, None] * BLOCK
    distance = ends - jnp.arange(BLOCK, dtype=jnp.int32)[None, :]
    bucket = sum((distance >= 2**k).astype(jnp.int32) for k in range(bucket_count - 1))
    rows = sum(
        jnp.where(bucket[None] == b, recency_bias[:, b][:, None, None], 0.0)
        for b in range(bucket_count)
    )
    past = jnp.full((recency_bias.shape[0], 1, BLOCK), MASKED, jnp.float32)
    return jnp.concatenate([past, rows * 0.5], axis=1)


def attend_kernel(cache_count, heads, pick, queries, own, other, table, out):
    rows, width = queries.shape
    size = width // heads
    events = own.shape[3]
    chunk = min(2 * BLOCK, events)
    blocks_used = pick[1]
    for head in range(heads):
        columns = slice(head * size, (head + 1) * size)
        query = queries[:, columns]
        total = jnp.zeros((rows, size), jnp.float32)
        for place, page in ((2, own), (3, other)):
            shift = pick[place]
            for first in range(0, events, chunk):
                bias = []
                for block in range(first // BLOCK, (first + chunk) // BLOCK):
                    left = jnp.maximum(blocks_used - (block * cache_count + shift), 0)
                    bias.append(table[head, pl.ds(left, 1), :])
                bias = jnp.concatenate(bias, axis=1)
                keys = page[0, 0, 0, first : first + chunk, columns]
                values = page[0, 0, 1, first : first + chunk, columns]
                half = (
                    lax.dot_general(
                        query, keys, (((1,), (1,)), ((), ())), preferred_element_type=jnp.float32
                    )
                    + bias
                )
                weights = (half + half * jnp.tanh(half)).astype(jnp.bfloat16)
                total = total + jnp.dot(weights, values, preferred_element_type=jnp.float32)
        out[:, columns] = total.astype(jnp.bfloat16)


def attend(cache_count, pick, queries, own, other, table):
    rows, width = queries.shape
    heads = table.shape[0]
    events = own.shape[3]
    tile = min(256, rows)
    return pl.pallas_call(
        functools.partial(attend_kernel, cache_count, heads),
        grid_spec=pltpu.PrefetchScalarGridSpec(
            num_scalar_prefetch=1,
            grid=(rows // tile,),
            in_specs=[
                pl.BlockSpec((tile, width), lambda i, s: (i, 0)),
                pl.BlockSpec((1, 1, 2, events, width), lambda i, s: (0, s[0], 0, 0, 0)),
                pl.BlockSpec((1, 1, 2, events, width), lambda i, s: (0, 0, 0, 0, 0)),
                pl.BlockSpec(table.shape, lambda i, s: (0, 0, 0)),
            ],
            out_specs=pl.BlockSpec((tile, width), lambda i, s: (i, 0)),
        ),
        out_shape=jax.ShapeDtypeStruct((rows, width), jnp.bfloat16),
        compiler_params=params(),
        cost_estimate=pl.CostEstimate(
            flops=8 * rows * width * events,
            bytes_accessed=4 * rows * width + 8 * events * width,
            transcendentals=2 * rows * heads * events,
        ),
        name="attend",
    )(pick, queries, own, other, table)


def project_kernel(scales, count, *refs):
    blocks, weight, outs = refs[:count], refs[count], refs[count + 1 :]
    rows = blocks[0].shape[0]
    width = outs[0].shape[1]
    for i, block in enumerate(blocks):
        normed = block[...]
        for kind, (scale, out) in enumerate(zip(scales, outs)):
            product = jnp.dot(
                normed,
                weight[:, kind * width : (kind + 1) * width],
                preferred_element_type=jnp.float32,
            )
            half = product * 0.5
            out[i * rows : (i + 1) * rows, :] = (
                (half + half * jnp.tanh(half)) * scale
            ).astype(jnp.bfloat16)


def project(scales, blocks, weight):
    rows, depth = blocks[0].shape
    width = weight.shape[1] // len(scales)
    total = rows * len(blocks)
    shape = jax.ShapeDtypeStruct((total, width), jnp.bfloat16)
    return pl.pallas_call(
        functools.partial(project_kernel, scales, len(blocks)),
        out_shape=[shape] * len(scales),
        compiler_params=params(),
        cost_estimate=pl.CostEstimate(
            flops=2 * total * depth * weight.shape[1],
            bytes_accessed=2 * total * depth + 2 * depth * weight.shape[1],
            transcendentals=total * weight.shape[1],
        ),
        name="project",
    )(*blocks, weight)


def finish_kernel(count, first_bias, *refs):
    parts, (gates, values, queries, keys, out) = refs[:count], refs[count:]
    heads = first_bias.shape[0]
    size = gates.shape[1] // heads
    for head in range(heads):
        columns = slice(head * size, (head + 1) * size)
        total = sum(part[:, columns].astype(jnp.float32) for part in parts)
        half = (
            jnp.sum(
                queries[:, columns].astype(jnp.float32) * keys[:, columns].astype(jnp.float32),
                axis=-1,
                keepdims=True,
            )
            + first_bias[head] * 0.5
        )
        total = total + (half + half * jnp.tanh(half)) * values[:, columns].astype(jnp.float32)
        scale = lax.rsqrt(jnp.mean(total * total, axis=-1, keepdims=True) + EPSILON)
        out[:, columns] = (total * scale * gates[:, columns].astype(jnp.float32)).astype(
            jnp.bfloat16
        )


def finish(first_bias, parts, gates, values, queries, keys):
    rows, width = gates.shape
    tile = min(256, rows)
    spec = pl.BlockSpec((tile, width), lambda i: (i, 0))
    return pl.pallas_call(
        functools.partial(finish_kernel, len(parts)),
        grid=(rows // tile,),
        in_specs=[pl.BlockSpec(memory_space=pltpu.SMEM)] + [spec] * (len(parts) + 4),
        out_specs=spec,
        out_shape=jax.ShapeDtypeStruct((rows, width), jnp.bfloat16),
        compiler_params=params(),
        name="finish",
    )(first_bias, *parts, gates, values, queries, keys)


def combine_kernel(count, states, score_weight, *refs):
    gated, weights, (layer, scores) = refs[:count], refs[count : 2 * count], refs[2 * count :]
    total = states[...].astype(jnp.float32)
    for part, weight in zip(gated, weights):
        total = total + jnp.dot(part[...], weight[...], preferred_element_type=jnp.float32)
    layer[...] = total.astype(jnp.bfloat16)
    scores[...] = jnp.sum(total * score_weight[...], axis=-1, keepdims=True)


def combine(states, score_weight, gated, weights):
    rows, width = states.shape
    return pl.pallas_call(
        functools.partial(combine_kernel, len(gated)),
        out_shape=[
            jax.ShapeDtypeStruct((rows, width), jnp.bfloat16),
            jax.ShapeDtypeStruct((rows, 1), jnp.float32),
        ],
        compiler_params=params(),
        name="combine",
    )(states, score_weight[None], *gated, *weights)


def swap(axis, bit):
    return functools.partial(
        lax.ppermute, axis_name=axis, perm=[(i, i ^ bit) for i in range(lax.axis_size(axis))]
    )


def local(
    cand_states, in_proj, out_proj, history, lengths, rank_users, recency_bias, score_weight
):
    cache_count = lax.axis_size("cache")
    place = lax.axis_index("cache")
    cand_rows, users_here, width = cand_states.shape
    head_width = in_proj.shape[2]
    heads = recency_bias.shape[0]
    events = history.shape[3]
    half_scale = 0.5 * (head_width // heads) ** (-0.5)

    swap_core, swap_chip = swap("cand", 1), swap("cand", 2)
    swap_both = swap("cand", 3)
    swap_page = swap("cache", 1)

    states = jnp.moveaxis(cand_states, 1, 0)
    floats = states.astype(jnp.float32)
    normed = (
        floats * lax.rsqrt(jnp.mean(floats * floats, axis=-1, keepdims=True) + EPSILON)
    ).astype(jnp.bfloat16)
    in_matrix = in_proj.reshape(width, 4 * head_width)
    query_weight = in_matrix[:, 2 * head_width : 3 * head_width]
    table = bias_rows(recency_bias, cache_count * events // BLOCK)
    first_bias = recency_bias[:, 0]

    def slot_user(index, member):
        return lax.dynamic_index_in_dim(rank_users, index * users_here + member, 0, False)

    def page_of(user):
        return lax.dynamic_slice_in_dim(history, user, 1, 1)

    def pick_of(user, first, second):
        used = lax.dynamic_index_in_dim(lengths, user, 0, False) // BLOCK
        return jnp.stack(
            [user, used, jnp.remainder(first - user, cache_count), jnp.remainder(second - user, cache_count)]
        ).astype(jnp.int32)

    def gather_rows(member):
        mine = normed[member]
        across = swap_chip(mine)
        near = swap_core(mine)
        return [mine, near, across, swap_core(across)]

    def spread(gated):
        pieces = gated.reshape(4, cand_rows, head_width)
        return [pieces[0], swap_core(pieces[1]), swap_chip(pieces[2]), swap_both(pieces[3])]

    weight_rows = None

    if cache_count == 8 and users_here == 2:
        line = place // 2
        lane = place % 2
        at_end = (line == 0) | (line == 3)
        exchange_outer = swap("cache", 2)
        exchange_inner = functools.partial(
            lax.ppermute, axis_name="cache", perm=[(2, 4), (4, 2), (3, 5), (5, 3)]
        )
        visits = jnp.array(
            [
                [0, 1, 2, 3, 3, 2, 1, 0],
                [1, 2, 3, 0, 3, 2, 0, 1],
                [2, 1, 0, 3, 0, 1, 3, 2],
                [3, 2, 1, 0, 0, 1, 2, 3],
            ],
            jnp.int32,
        )
        visited = lax.dynamic_index_in_dim(visits, line, 0, False)
        members = (0, 0, 0, 0, 1, 1, 1, 1)
        picks, sent = [], []
        for step in range(8):
            user = slot_user(visited[step] * 2 + lane, members[step])
            picks.append(pick_of(user, place, place ^ 1))
            sent.append(slot_user(visited[step] * 2 + 1 - lane, members[step]))

        def partial_totals(step, queries, page):
            return attend(cache_count, picks[step], queries, history, page, table)

        def either(first, second):
            return jnp.where(at_end, first, second)

        pages = [swap_page(page_of(sent[0]))]
        rows_a = gather_rows(0)
        (query_a,) = project((half_scale,), rows_a, query_weight)
        page_next, query_a, rows_a[0] = tied(page_of(sent[1]), query_a, rows_a[0])
        pages.append(swap_page(page_next))
        rows_b = gather_rows(1)
        others_weight = jnp.concatenate(
            [in_matrix[:, : 2 * head_width], in_matrix[:, 3 * head_width :]], axis=1
        )

        outer, inner, totals = [], [], []
        to_outer, to_inner, queries = query_a, query_a, query_a
        for step in range(8):
            outer.append(exchange_outer(to_outer))
            inner.append(exchange_inner(to_inner))
            if step + 2 < 8:
                pages.append(swap_page(page_of(sent[step + 2])))
            totals.append(partial_totals(step, queries, pages[step]))
            if step == 0:
                (query_b,) = project((half_scale,), rows_b, query_weight)
                query_b, out_mine = tied(query_b, out_proj)
            if step == 1:
                rows_a = list(tied(*rows_a))
                gates_a, values_a, keys_a = project((1.0, 1.0, 1.0), rows_a, others_weight)
                out_across = swap_chip(out_mine)
            if step == 2:
                rows_b = list(tied(*rows_b))
                gates_b, values_b, keys_b = project((1.0, 1.0, 1.0), rows_b, others_weight)
                weight_rows = [out_mine, swap_core(out_mine), out_across, swap_core(out_across)]
            if step == 7:
                break
            outer[step], inner[step], totals[step], pages[-1] = tied(
                outer[step], inner[step], totals[step], pages[-1]
            )
            if step == 0:
                to_outer, to_inner = either(query_b, inner[0]), outer[0]
                queries = either(outer[0], inner[0])
            if step == 1:
                to_outer, to_inner = either(totals[1], inner[1]), outer[1]
                queries = either(outer[1], inner[1])
            if step == 2:
                to_outer, to_inner = either(totals[2], inner[2]), query_b
                queries = either(outer[2], outer[0])
            if step == 3:
                to_outer, to_inner = either(totals[3], inner[3]), outer[3] + totals[1]
                queries = either(outer[3], inner[2])
            if step == 4:
                to_outer, to_inner = either(totals[4], query_b), outer[4] + totals[2]
                queries = either(outer[4], inner[3])
            if step == 5:
                to_outer, to_inner = either(totals[5], inner[5] + totals[3]), outer[5] + totals[4]
                queries = either(outer[5], outer[1])
            if step == 6:
                to_outer, to_inner = either(totals[6], inner[6] + totals[6]), outer[6] + totals[5]
                queries = query_b
                zero = jnp.zeros_like(totals[0])
                gated_a = finish(
                    first_bias,
                    [totals[0], either(outer[6], outer[2]), inner[4]],
                    gates_a, values_a, query_a, keys_a,
                )
                spread_a = spread(gated_a)
        layer_a, scores_a = combine(states[0], score_weight, spread_a, weight_rows)
        gated_b = finish(
            first_bias, [totals[7], outer[7], inner[7]], gates_b, values_b, query_b, keys_b
        )
        layer_b, scores_b = combine(states[1], score_weight, spread(gated_b), weight_rows)
        return (
            jnp.stack([layer_a, layer_b], axis=1),
            jnp.concatenate([scores_a, scores_b], axis=1),
        )

    chosen = jnp.take(history[0], rank_users, axis=0).reshape(
        cache_count, users_here, 2, events, head_width
    )
    arrived = lax.all_to_all(chosen, "cache", split_axis=0, concat_axis=0, tiled=True)
    out_across = swap_chip(out_proj)
    weight_rows = [out_proj, swap_core(out_proj), out_across, swap_core(out_across)]
    layers, scores = [], []
    for member in range(users_here):
        user = slot_user(place, member)
        gates, values, queries, keys = project(
            (1.0, 1.0, half_scale, 1.0), gather_rows(member), in_matrix
        )

        def add_pair(step, total, user=user, member=member, queries=queries):
            pair = lax.dynamic_slice(
                arrived, (2 * step, member, 0, 0, 0), (2, 1, 2, events, head_width)
            )
            pick = pick_of(user, 2 * step, 2 * step + 1).at[0].set(0)
            part = attend(cache_count, pick, queries, pair[:1], pair[1:], table)
            return total + part.astype(jnp.float32)

        total = lax.fori_loop(
            0, cache_count // 2, add_pair, jnp.zeros(queries.shape, jnp.float32)
        )
        gated = finish(first_bias, [total], gates, values, queries, keys)
        layer, score = combine(states[member], score_weight, spread(gated), weight_rows)
        layers.append(layer)
        scores.append(score)
    return jnp.stack(layers, axis=1), jnp.concatenate(scores, axis=1)


def solution(mesh):
    in_specs = (
        P("cand", "cache", None),
        P(None, None, "cand"),
        P("cand", None),
        P("cache", None, None, None, "cand"),
        P(),
        P(),
        P("cand", None),
        P(),
    )
    out_specs = (P("cand", "cache", None), P("cand", "cache"))
    return jax.shard_map(local, mesh=mesh, in_specs=in_specs, out_specs=out_specs, check_vma=False)
```

```python
import functools
import math

import jax
import jax.numpy as jnp
from jax import lax
from jax.experimental import pallas as pl
from jax.experimental.pallas import tpu as pltpu
from jax.sharding import PartitionSpec as P

BLOCK = 128
EPSILON = 1e-06
MASKED = -1e30
MIB = 1024 * 1024


def local_call(kernel, name, args, outs, flops=0, scratch=(), places=(), held=True):
    places = dict(places)
    placed = [
        arg
        if places.get(i) == pltpu.SMEM
        else pltpu.with_memory_space_constraint(arg, places.get(i, pltpu.VMEM))
        for i, arg in enumerate(args)
    ]
    return pl.pallas_call(
        kernel,
        in_specs=[
            pl.BlockSpec(memory_space=places.get(i, pltpu.VMEM)) for i in range(len(args))
        ],
        out_specs=[pl.BlockSpec(memory_space=pltpu.VMEM)] * len(outs),
        out_shape=[
            pltpu.VMEM(shape, dtype) if held else jax.ShapeDtypeStruct(shape, dtype)
            for shape, dtype in outs
        ],
        scratch_shapes=list(scratch),
        compiler_params=pltpu.CompilerParams(vmem_limit_bytes=20 * MIB),
        cost_estimate=pl.CostEstimate(
            flops=flops,
            bytes_accessed=sum(math.prod(shape) for shape, _ in outs) * 2,
            transcendentals=0,
        ),
        name=name,
    )(*placed)


def tied(*arrays):
    return lax.optimization_barrier(arrays)


def bias_rows(recency_bias, most_blocks):
    bucket_count = recency_bias.shape[1]
    ends = jnp.arange(1, most_blocks + 1, dtype=jnp.int32)[:, None] * BLOCK
    distance = ends - jnp.arange(BLOCK, dtype=jnp.int32)[None, :]
    bucket = sum((distance >= 2**k).astype(jnp.int32) for k in range(bucket_count - 1))
    rows = sum(
        jnp.where(bucket[None] == b, recency_bias[:, b][:, None, None], 0.0)
        for b in range(bucket_count)
    )
    past = jnp.full((recency_bias.shape[0], 1, BLOCK), MASKED, jnp.float32)
    return jnp.concatenate([past, rows * 0.5], axis=1)


def attend_kernel(cache_count, step, member, halves, sends, picks, history, other, table, *refs):
    refs, (query, own, sem, next_sem) = refs[:-4], refs[-4:]
    queries, (out, *next_page) = (refs[:-2], refs[-2:]) if sends else (refs[:-1], refs[-1:])
    heads = table.shape[0]
    rows, width = out.shape
    size = width // heads
    blocks = own.shape[1] // BLOCK
    user, blocks_used, *shifts, which, next_user = (picks[6 * step + i] for i in range(6))
    fetch = pltpu.make_async_copy(history.at[0, user], own, sem)
    fetch.start()
    if sends:
        next_fetch = pltpu.make_async_copy(history.at[0, next_user], next_page[0].at[0], next_sem)
        next_fetch.start()
    if len(queries) == halves:
        for i, ref in enumerate(queries):
            query[i * rows // halves : (i + 1) * rows // halves, :] = ref[...]
    else:
        for i, (first, second) in enumerate(zip(queries[:halves], queries[halves:])):
            query[i * rows // halves : (i + 1) * rows // halves, :] = jnp.where(
                which == 0, first[...], second[...]
            )

    def part(page, head, shift, first, count):
        left = [
            jnp.maximum(blocks_used - (block * cache_count + shift), 0)
            for block in range(first, first + count)
        ]
        bias = jnp.concatenate([table[head, pl.ds(m, 1), :] for m in left], axis=1)
        events = slice(first * BLOCK, (first + count) * BLOCK)
        columns = slice(head * size, (head + 1) * size)
        half = bias + lax.dot_general(
            query[:, columns],
            page[0, events, columns],
            (((1,), (1,)), ((), ())),
            preferred_element_type=jnp.float32,
        )
        weights = (half + half * jnp.tanh(half)).astype(jnp.bfloat16)
        return jnp.dot(weights, page[1, events, columns], preferred_element_type=jnp.float32)

    needed = jnp.maximum(blocks_used - jnp.minimum(*shifts) + cache_count - 1, 0) // cache_count
    least = (blocks + 1) // 2
    for used in range(least, blocks + 1):
        fits = needed == used
        if used == least:
            fits = needed <= used
        if used == blocks:
            fits = needed >= used

        @pl.when(fits)
        def _(used=used):
            firsts = range(0, used, 2)
            totals = [
                sum(
                    part(other.at[member], head, shifts[1], first, min(2, used - first))
                    for first in firsts
                )
                for head in range(heads)
            ]
            fetch.wait()
            for head, total in enumerate(totals):
                total = total + sum(
                    part(own, head, shifts[0], first, min(2, used - first)) for first in firsts
                )
                out[:, head * size : (head + 1) * size] = total.astype(jnp.bfloat16)

    if sends:
        next_fetch.wait()


def attend(cache_count, picks, step, queries, history, other, member, table, sends=False):
    halves = len(queries[0])
    queries = [piece for array in queries for piece in array]
    rows, width = halves * queries[0].shape[0], queries[0].shape[1]
    outs = [((rows, width), jnp.bfloat16), ((1,) + history.shape[2:], history.dtype)]
    return local_call(
        functools.partial(attend_kernel, cache_count, step, member, halves, sends),
        "attend",
        [picks, history, other, table, *queries],
        outs if sends else outs[:1],
        flops=16 * rows * width * history.shape[3],
        scratch=[
            pltpu.VMEM((rows, width), jnp.bfloat16),
            pltpu.VMEM(history.shape[2:], history.dtype),
            pltpu.SemaphoreType.DMA,
            pltpu.SemaphoreType.DMA,
        ],
        places={0: pltpu.SMEM, 1: pltpu.HBM},
    )


def pages_kernel(count, users, history, out, sem):
    rows = min(2 * BLOCK, history.shape[3])
    copies = [
        pltpu.make_async_copy(
            history.at[0, users[i], kind, pl.ds(first, rows)],
            out.at[i, kind, pl.ds(first, rows)],
            sem.at[i, kind, first // rows],
        )
        for i in range(count)
        for kind in range(2)
        for first in range(0, history.shape[3], rows)
    ]
    for copy in copies:
        copy.start()
    for copy in copies:
        copy.wait()


def pages_of(users, count, history):
    (pages,) = local_call(
        functools.partial(pages_kernel, count),
        "pages",
        [users, history],
        [((count,) + history.shape[2:], history.dtype)],
        scratch=[pltpu.SemaphoreType.DMA((count, 2, max(1, history.shape[3] // (2 * BLOCK))))],
        places={0: pltpu.SMEM, 1: pltpu.HBM},
    )
    return pages


def behind_kernel(scale, weight, first, second, ahead, out):
    rows = ahead.shape[0]
    out[:rows, :] = ahead[...]
    project_kernel([(2, scale)], 1, 2, weight, first, second, out.at[pl.ds(rows, rows)])


def project_behind(ahead, scale, blocks, in_matrix):
    rows, width = ahead.shape
    (queries,) = local_call(
        functools.partial(behind_kernel, scale),
        "project",
        [in_matrix, *blocks, ahead],
        [((2 * rows, width), jnp.bfloat16)],
        flops=2 * rows * math.prod(in_matrix.shape) // 4,
    )
    return queries


def project_kernel(kinds, groups, count, weight, *refs):
    blocks, outs = refs[:count], refs[count:]
    rows = blocks[0].shape[0]
    width = outs[0].shape[1]
    in_group = count // groups
    for i, block in enumerate(blocks):
        group, place = divmod(i, in_group)
        state = block[...].astype(jnp.float32)
        normed = (
            state * lax.rsqrt(jnp.mean(state * state, axis=-1, keepdims=True) + EPSILON)
        ).astype(jnp.bfloat16)
        for (quarter, scale), out in zip(kinds, outs[group * len(kinds) :]):
            half = 0.5 * jnp.dot(
                normed,
                weight[:, quarter * width : (quarter + 1) * width],
                preferred_element_type=jnp.float32,
            )
            out[place * rows : (place + 1) * rows, :] = (
                (half + half * jnp.tanh(half)) * scale
            ).astype(jnp.bfloat16)


def project(kinds, blocks, in_matrix, groups=1):
    rows = blocks[0].shape[0]
    shape = (rows * len(blocks) // groups, in_matrix.shape[1] // 4)
    return local_call(
        functools.partial(project_kernel, kinds, groups, len(blocks)),
        "project",
        [in_matrix, *blocks],
        [(shape, jnp.bfloat16)] * (len(kinds) * groups),
        flops=2 * rows * len(blocks) * in_matrix.shape[0] * shape[1] * len(kinds),
    )


def finish_kernel(half, count, first_bias, *refs):
    parts, heads_refs, outs = refs[:count], refs[count:-2], refs[-2:]
    gates, values, keys, *queries = heads_refs
    heads = first_bias.shape[0]
    rows, width = outs[0].shape
    size = width // heads

    def load(ref, i, columns):
        first = i * rows
        if ref.shape[0] == 4 * rows:
            first = first + half * 2 * rows
        return ref[first : first + rows, columns].astype(jnp.float32)

    for i, out in enumerate(outs):
        for head in range(heads):
            columns = slice(head * size, (head + 1) * size)
            total = sum(load(part, i, columns) for part in parts)
            products = load(queries[0], i, columns) * load(keys, i, columns)
            score = jnp.sum(products, axis=-1, keepdims=True) + first_bias[head] * 0.5
            total = total + (score + score * jnp.tanh(score)) * load(values, i, columns)
            scale = lax.rsqrt(jnp.mean(total * total, axis=-1, keepdims=True) + EPSILON)
            out[:, columns] = (total * scale * load(gates, i, columns)).astype(jnp.bfloat16)


def finish(first_bias, half, parts, gates, values, keys, query):
    rows, width = gates.shape
    return local_call(
        functools.partial(finish_kernel, half, len(parts)),
        "finish",
        [first_bias, *parts, gates, values, keys, *query],
        [((rows // 4, width), jnp.bfloat16)] * 2,
        places={0: pltpu.SMEM},
    )


def combine_kernel(count, states, score_weight, *refs):
    gated, weights, rest = refs[:count], refs[count : 2 * count], refs[2 * count :]
    *before, layer, scores = rest
    total = states[...].astype(jnp.float32)
    for part, weight in zip(gated, weights):
        total = total + jnp.dot(part[...], weight[...], preferred_element_type=jnp.float32)
    column = jnp.sum(total * score_weight[...], axis=-1, keepdims=True)
    row = jnp.transpose(jnp.broadcast_to(column, (column.shape[0], 128)))[:1]
    if before:
        layer[:, 0, :] = before[0][...]
        layer[:, 1, :] = total.astype(jnp.bfloat16)
        scores[:1, :] = before[1][...]
        scores[1:, :] = row
    else:
        layer[...] = total.astype(jnp.bfloat16)
        scores[...] = row


def combine(states, score_weight, gated, weights, before=()):
    rows, width = states.shape
    layer = (rows, 2, width) if before else (rows, width)
    return local_call(
        functools.partial(combine_kernel, len(gated)),
        "combine",
        [states, score_weight[None], *gated, *weights, *before],
        [(layer, jnp.bfloat16), ((2 if before else 1, rows), jnp.float32)],
        held=False,
    )


def swap(axis, bit):
    return functools.partial(
        lax.ppermute, axis_name=axis, perm=[(i, i ^ bit) for i in range(lax.axis_size(axis))]
    )


def local(
    cand_states, in_proj, out_proj, history, lengths, rank_users, recency_bias, score_weight
):
    cache_count = lax.axis_size("cache")
    place = lax.axis_index("cache")
    cand_rows, users_here, width = cand_states.shape
    head_width = in_proj.shape[2]
    heads = recency_bias.shape[0]
    events = history.shape[3]
    half_scale = 0.5 * (head_width // heads) ** (-0.5)

    swap_core, swap_chip = swap("cand", 1), swap("cand", 2)
    swap_both = swap("cand", 3)
    swap_page = swap("cache", 1)

    states = jnp.moveaxis(cand_states, 1, 0)
    in_matrix = in_proj.reshape(width, 4 * head_width)
    table = bias_rows(recency_bias, cache_count * events // BLOCK)
    first_bias = recency_bias[:, 0]

    def lookup(values, places):
        index = jnp.arange(values.shape[0], dtype=jnp.int32)
        return jnp.sum(jnp.where(places[:, None] == index, values, 0), axis=1)

    def picks_of(users, first, second, which, others):
        used = lookup(lengths, users) // BLOCK
        columns = [
            users, used, jnp.remainder(first - users, cache_count),
            jnp.remainder(second - users, cache_count), jnp.broadcast_to(which, users.shape), others,
        ]
        return jnp.stack(columns, axis=1).reshape(-1).astype(jnp.int32)

    def spread(near, far):
        return [near[0], swap_core(near[1]), swap_chip(far[0]), swap_both(far[1])]

    if cache_count == 8 and users_here == 2:
        line = [
            [0, 1, 2, 3, 3, 2, 1, 0],
            [1, 2, 3, 0, 3, 2, 0, 1],
            [2, 1, 0, 3, 0, 1, 3, 2],
            [3, 2, 1, 0, 0, 1, 2, 3],
        ]
        slots = [
            [(line[p // 2][k] * 2 + q) * 2 + k // 4 for q in (1 - p % 2, p % 2) for k in range(8)]
            for p in range(8)
        ]
        slots = lax.dynamic_index_in_dim(jnp.array(slots, jnp.int32), place, 0, False)
        users = lookup(rank_users, slots)
        at_end = (place < 2) | (place >= 6)
        exchange_outer = swap("cache", 2)
        exchange_inner = functools.partial(
            lax.ppermute, axis_name="cache", perm=[(2, 4), (4, 2), (3, 5), (5, 3)]
        )
        picks = picks_of(
            users[8:], place, place ^ 1, jnp.where(at_end, 0, 1), jnp.roll(users[:8], -2)
        )
        query_only = ((2, half_scale),)
        all_others = ((0, 1.0), (1, 1.0), (3, 1.0))

        def either(first, second):
            return jnp.where(at_end, first, second)

        def heads_of(step, queries, pages, member=0, sends=False):
            return attend(
                cache_count, picks, step, queries, history, pages, member, table, sends
            )

        mine_a, mine_b = states[0], states[1]
        across_a, near_a, near_b = swap_chip(mine_a), swap_core(mine_a), swap_core(mine_b)
        mine_b, near_a = tied(mine_b, near_a)
        across_b = swap_chip(mine_b)
        sending = pages_of(users[:2], 2, history)
        page = swap_page(sending[:1])
        query_near_a, query_near_b = project(
            query_only, [mine_a, near_a, mine_b, near_b], in_matrix, groups=2
        )
        across_a, query_near_a = tied(across_a, query_near_a)
        rows_a = [mine_a, near_a, across_a, swap_core(across_a)]
        query_a = project_behind(query_near_a, half_scale, rows_a[2:], in_matrix)
        query_a, sending = tied(query_a, sending[1:])

        outer, inner, totals = [], [], []
        for step in range(8):
            if step == 0:
                to_outer, to_inner, queries = query_a, query_a, [query_a]
            if step == 1:
                across_b, outer[0] = tied(across_b, outer[0])
                rows_b = [mine_b, near_b, across_b, swap_core(across_b)]
                query_b = project_behind(query_near_b, half_scale, rows_b[2:], in_matrix)
                to_outer, to_inner = either(query_b, inner[0]), outer[0]
                queries = [outer[0], inner[0]]
            if step == 2:
                to_outer, to_inner = either(totals[1], inner[1]), outer[1]
                queries = [outer[1], inner[1]]
            if step == 3:
                to_outer, to_inner = either(totals[2], inner[2]), query_b
                queries = [outer[2], outer[0]]
                to_outer, out_mine = tied(to_outer, out_proj)
            if step == 4:
                to_outer, to_inner = either(totals[3], inner[3]), outer[3] + totals[1]
                queries = [outer[3], inner[2]]
                out_mine, out_across, out_near = out_rows
                to_outer, out_across = tied(to_outer, out_across)
            if step == 5:
                to_outer, to_inner = either(totals[4], query_b), outer[4] + totals[2]
                queries = [outer[4], inner[3]]
            if step == 6:
                to_outer, to_inner = either(totals[5], inner[5] + totals[3]), outer[5] + totals[4]
                queries = [outer[5], outer[1]]
            if step == 7:
                to_outer, to_inner = either(totals[6], inner[6] + totals[6]), outer[6] + totals[5]
                queries = [query_b]
            outer.append(exchange_outer(to_outer))
            inner.append(exchange_inner(to_inner))
            held, page = page, swap_page(sending) if step < 7 else None
            total, *sending = heads_of(step, [[array] for array in queries], held, 0, step < 6)
            extra = []
            if step == 1:
                rows_a[0], total = tied(rows_a[0], total)
                extra = project(all_others, rows_a, in_matrix)
            if step == 2:
                rows_b[0], total = tied(rows_b[0], total)
                extra = project(all_others, rows_b, in_matrix)
            if step == 3:
                extra = [out_mine, swap_chip(out_mine), swap_core(out_mine)]
            if step == 4:
                extra = [out_mine, out_near, out_across, swap_core(out_across)]
            if step == 7:
                parts_a = [totals[0], either(outer[6], outer[2]), inner[4]]
                far_a = finish(first_bias, 1, parts_a, *heads_a)
                near_a = finish(first_bias, 0, parts_a, *heads_a)
                extra = combine(states[0], score_weight, spread(near_a, far_a), out_rows)
            outer[step], inner[step], total, *rest = tied(
                outer[step], inner[step], total, *sending, *extra
            )
            totals.append(total)
            if sending:
                sending, *extra = rest
            else:
                extra = rest
            if step == 1:
                heads_a = (*extra, [query_a])
            if step == 2:
                heads_b = (*extra, [query_b])
            if step in (3, 4):
                out_rows = extra
        parts_b = [totals[7], outer[7], inner[7]]
        far_b = finish(first_bias, 1, parts_b, *heads_b)
        near_b = finish(first_bias, 0, parts_b, *heads_b)
        layer, scores = combine(
            states[1], score_weight, spread(near_b, far_b), out_rows, extra
        )
        return layer, scores.T

    chosen = jnp.take(history[0], rank_users, axis=0).reshape(
        cache_count, users_here, 2, events, head_width
    )
    arrived = lax.all_to_all(chosen, "cache", split_axis=0, concat_axis=0, tiled=True)
    out_across = swap_chip(out_proj)
    weight_rows = [out_proj, swap_core(out_proj), out_across, swap_core(out_across)]
    my_users = lax.dynamic_slice_in_dim(rank_users, place * users_here, users_here)
    layers, scores = [], []
    for member in range(users_here):
        across = swap_chip(states[member])
        rows = [states[member], swap_core(states[member]), across, swap_core(across)]
        kinds = ((0, 1.0), (1, 1.0), (2, half_scale), (3, 1.0))
        gates, values, queries, keys = project(kinds, rows, in_matrix)

        def add_pair(step, total, member=member, queries=queries):
            pair = lax.dynamic_slice(
                arrived, (2 * step, member, 0, 0, 0), (2, 1, 2, events, head_width)
            )
            user = my_users[member][None]
            picks = picks_of(user, 2 * step, 2 * step + 1, 0, user).at[0].set(0)
            (part,) = attend(cache_count, picks, 0, [[queries]], pair[:1], pair[1:, 0], 0, table)
            return total + part.astype(jnp.float32)

        total = lax.fori_loop(
            0, cache_count // 2, add_pair, jnp.zeros(queries.shape, jnp.float32)
        )
        near, far = (
            finish(first_bias, half, [total], gates, values, keys, [queries]) for half in (0, 1)
        )
        layer, score = combine(states[member], score_weight, spread(near, far), weight_rows)
        layers.append(layer)
        scores.append(score)
    return jnp.stack(layers, axis=1), jnp.concatenate(scores, axis=0).T


def solution(mesh):
    in_specs = (
        P("cand", "cache", None),
        P(None, None, "cand"),
        P("cand", None),
        P("cache", None, None, None, "cand"),
        P(),
        P(),
        P("cand", None),
        P(),
    )
    out_specs = (P("cand", "cache", None), P("cand", "cache"))
    return jax.shard_map(local, mesh=mesh, in_specs=in_specs, out_specs=out_specs, check_vma=False)
```

```python
import functools

import jax
import jax.numpy as jnp
from jax import lax
from jax.experimental import pallas as pl
from jax.experimental.pallas import tpu as pltpu
from jax.sharding import PartitionSpec as P

BLOCK = 128
EPSILON = 1e-06
MASKED = -1e30
MIB = 1024 * 1024
QUICK = pl.CostEstimate(flops=1, bytes_accessed=1, transcendentals=0)


def local_call(kernel, name, args, outs, scratch=(), places=(), held=True):
    places = dict(places)
    placed = [
        arg
        if places.get(i) == pltpu.SMEM
        else pltpu.with_memory_space_constraint(arg, places.get(i, pltpu.VMEM))
        for i, arg in enumerate(args)
    ]
    return pl.pallas_call(
        kernel,
        in_specs=[
            pl.BlockSpec(memory_space=places.get(i, pltpu.VMEM)) for i in range(len(args))
        ],
        out_specs=[pl.BlockSpec(memory_space=pltpu.VMEM)] * len(outs),
        out_shape=[
            pltpu.VMEM(shape, dtype) if held else jax.ShapeDtypeStruct(shape, dtype)
            for shape, dtype in outs
        ],
        scratch_shapes=list(scratch),
        compiler_params=pltpu.CompilerParams(vmem_limit_bytes=20 * MIB),
        cost_estimate=QUICK,
        name=name,
    )(*placed)


def tied(*arrays):
    return lax.optimization_barrier(arrays)


def bias_rows(recency_bias, most_blocks):
    bucket_count = recency_bias.shape[1]
    ends = jnp.arange(1, most_blocks + 1, dtype=jnp.int32)[:, None] * BLOCK
    distance = ends - jnp.arange(BLOCK, dtype=jnp.int32)[None, :]
    bucket = sum((distance >= 2**k).astype(jnp.int32) for k in range(bucket_count - 1))
    rows = sum(
        jnp.where(bucket[None] == b, recency_bias[:, b][:, None, None], 0.0)
        for b in range(bucket_count)
    )
    past = jnp.full((recency_bias.shape[0], 1, BLOCK), MASKED, jnp.float32)
    return jnp.concatenate([past, rows * 0.5], axis=1)


def attend_kernel(cache_count, step, member, halves, sends, picks, history, other, table, *refs):
    refs, (query, own, totals, sem, next_sem) = refs[:-5], refs[-5:]
    queries, (out, *next_page) = (refs[:-2], refs[-2:]) if sends else (refs[:-1], refs[-1:])
    heads = table.shape[0]
    rows, width = out.shape
    size = width // heads
    blocks = own.shape[1] // BLOCK
    user, blocks_used, *shifts, which, next_user = (picks[6 * step + i] for i in range(6))
    fetch = pltpu.make_async_copy(history.at[0, user], own, sem)
    fetch.start()
    if sends:
        next_fetch = pltpu.make_async_copy(history.at[0, next_user], next_page[0].at[0], next_sem)
        next_fetch.start()
    if len(queries) == halves:
        for i, ref in enumerate(queries):
            query[i * rows // halves : (i + 1) * rows // halves, :] = ref[...]
    else:
        for i, (first, second) in enumerate(zip(queries[:halves], queries[halves:])):
            query[i * rows // halves : (i + 1) * rows // halves, :] = jnp.where(
                which == 0, first[...], second[...]
            )

    def add_blocks(page, shift, first, count):
        left = [jnp.maximum(blocks_used - ((first + i) * cache_count + shift), 0) for i in range(count)]
        events = pl.ds(pl.multiple_of(first * BLOCK, BLOCK), count * BLOCK)
        for head in range(heads):
            columns = slice(head * size, (head + 1) * size)
            bias = jnp.concatenate([table[head, pl.ds(m, 1), :] for m in left], axis=1)
            half = bias + lax.dot_general(
                query[:, columns],
                page[0, events, columns],
                (((1,), (1,)), ((), ())),
                preferred_element_type=jnp.float32,
            )
            weights = (half + half * jnp.tanh(half)).astype(jnp.bfloat16)
            totals[:, columns] += jnp.dot(
                weights, page[1, events, columns], preferred_element_type=jnp.float32
            )

    needed = jnp.maximum(blocks_used - jnp.minimum(*shifts) + cache_count - 1, 0) // cache_count
    needed = jnp.minimum(needed, blocks)
    pairs = needed // 2

    def add_page(page, shift):
        def add_pair(pair, carry):
            add_blocks(page, shift, 2 * pair, 2)
            return carry

        if blocks > 1:
            lax.fori_loop(0, pairs, add_pair, 0)

        @pl.when(needed > 2 * pairs)
        def _():
            add_blocks(page, shift, 2 * pairs, 1)

    totals[...] = jnp.zeros_like(totals)
    add_page(other.at[member], shifts[1])
    fetch.wait()
    add_page(own, shifts[0])
    out[...] = totals[...].astype(jnp.bfloat16)

    if sends:
        next_fetch.wait()


def attend(cache_count, picks, step, queries, history, other, member, table, sends=False):
    halves = len(queries[0])
    queries = [piece for array in queries for piece in array]
    rows, width = halves * queries[0].shape[0], queries[0].shape[1]
    outs = [((rows, width), jnp.bfloat16), ((1,) + history.shape[2:], history.dtype)]
    return local_call(
        functools.partial(attend_kernel, cache_count, step, member, halves, sends),
        "attend",
        [picks, history, other, table, *queries],
        outs if sends else outs[:1],
        scratch=[
            pltpu.VMEM((rows, width), jnp.bfloat16),
            pltpu.VMEM(history.shape[2:], history.dtype),
            pltpu.VMEM((rows, width), jnp.float32),
            pltpu.SemaphoreType.DMA,
            pltpu.SemaphoreType.DMA,
        ],
        places={0: pltpu.SMEM, 1: pltpu.HBM},
    )


def pages_kernel(users, history, *refs):
    outs, sem = refs[:-1], refs[-1]
    rows = min(2 * BLOCK, history.shape[3])
    copies = [
        pltpu.make_async_copy(
            history.at[0, users[i], kind, pl.ds(first, rows)],
            out.at[0, kind, pl.ds(first, rows)],
            sem.at[i, kind, first // rows],
        )
        for i, out in enumerate(outs)
        for kind in range(2)
        for first in range(0, history.shape[3], rows)
    ]
    for copy in copies:
        copy.start()
    for copy in copies:
        copy.wait()


def pages_of(users, count, history):
    return local_call(
        pages_kernel,
        "pages",
        [users, history],
        [((1,) + history.shape[2:], history.dtype)] * count,
        scratch=[pltpu.SemaphoreType.DMA((count, 2, max(1, history.shape[3] // (2 * BLOCK))))],
        places={0: pltpu.SMEM, 1: pltpu.HBM},
    )


def behind_kernel(scale, weight, ahead, *refs):
    *blocks, out = refs
    rows = ahead.shape[0]
    out[:rows, :] = ahead[...]
    project_kernel(
        [(2, scale)], 1, len(blocks), weight, *blocks, out.at[pl.ds(rows, rows)]
    )


def project_behind(ahead, scale, blocks, in_matrix):
    rows, width = ahead.shape
    (queries,) = local_call(
        functools.partial(behind_kernel, scale),
        "project",
        [in_matrix, ahead, *blocks],
        [((2 * rows, width), jnp.bfloat16)],
    )
    return queries


def project_kernel(kinds, groups, count, weight, *refs):
    blocks, outs = refs[:count], refs[count:]
    total, width = outs[0].shape
    first, group = 0, 0
    for block in blocks:
        rows = block.shape[0]
        state = block[...].astype(jnp.float32)
        half_norm = 0.5 * lax.rsqrt(jnp.mean(state * state, axis=-1, keepdims=True) + EPSILON)
        for (quarter, scale), out in zip(kinds, outs[group * len(kinds) :]):
            half = half_norm * jnp.dot(
                block[...],
                weight[:, quarter * width : (quarter + 1) * width],
                preferred_element_type=jnp.float32,
            )
            out[first : first + rows, :] = (
                (half + half * jnp.tanh(half)) * scale
            ).astype(jnp.bfloat16)
        first += rows
        if first == total:
            first, group = 0, group + 1


def project(kinds, blocks, in_matrix, groups=1):
    shape = (sum(block.shape[0] for block in blocks) // groups, in_matrix.shape[1] // 4)
    return local_call(
        functools.partial(project_kernel, kinds, groups, len(blocks)),
        "project",
        [in_matrix, *blocks],
        [(shape, jnp.bfloat16)] * (len(kinds) * groups),
    )


def finish_kernel(half, count, first_bias, *refs):
    parts, heads_refs, outs = refs[:count], refs[count:-2], refs[-2:]
    gates, values, keys, *queries = heads_refs
    heads = first_bias.shape[0]
    rows, width = outs[0].shape
    size = width // heads

    def load(ref, i, columns):
        first = i * rows
        if ref.shape[0] == 4 * rows:
            first = first + half * 2 * rows
        return ref[first : first + rows, columns].astype(jnp.float32)

    for i, out in enumerate(outs):
        for head in range(heads):
            columns = slice(head * size, (head + 1) * size)
            total = sum(load(part, i, columns) for part in parts)
            products = load(queries[0], i, columns) * load(keys, i, columns)
            score = jnp.sum(products, axis=-1, keepdims=True) + first_bias[head] * 0.5
            total = total + (score + score * jnp.tanh(score)) * load(values, i, columns)
            scale = lax.rsqrt(jnp.mean(total * total, axis=-1, keepdims=True) + EPSILON)
            out[:, columns] = (total * scale * load(gates, i, columns)).astype(jnp.bfloat16)


def finish(first_bias, half, parts, gates, values, keys, query):
    rows, width = gates.shape
    return local_call(
        functools.partial(finish_kernel, half, len(parts)),
        "finish",
        [first_bias, *parts, gates, values, keys, *query],
        [((rows // 4, width), jnp.bfloat16)] * 2,
        places={0: pltpu.SMEM},
    )


def combine_kernel(count, states, score_weight, *refs):
    gated, weights, rest = refs[:count], refs[count : 2 * count], refs[2 * count :]
    *before, layer, scores = rest
    total = states[...].astype(jnp.float32)
    for part, weight in zip(gated, weights):
        total = total + jnp.dot(part[...], weight[...], preferred_element_type=jnp.float32)
    column = jnp.sum(total * score_weight[...], axis=-1, keepdims=True)
    row = jnp.transpose(jnp.broadcast_to(column, (column.shape[0], 128)))[:1]
    if before:
        layer[:, 0, :] = before[0][...]
        layer[:, 1, :] = total.astype(jnp.bfloat16)
        scores[:1, :] = before[1][...]
        scores[1:, :] = row
    else:
        layer[...] = total.astype(jnp.bfloat16)
        scores[...] = row


def combine(states, score_weight, gated, weights, before=()):
    rows, width = states.shape
    layer = (rows, 2, width) if before else (rows, width)
    return local_call(
        functools.partial(combine_kernel, len(gated)),
        "combine",
        [states, score_weight[None], *gated, *weights, *before],
        [(layer, jnp.bfloat16), ((2 if before else 1, rows), jnp.float32)],
        held=False,
    )


def swap(axis, bit):
    return functools.partial(
        lax.ppermute, axis_name=axis, perm=[(i, i ^ bit) for i in range(lax.axis_size(axis))]
    )


def local(
    cand_states, in_proj, out_proj, history, lengths, rank_users, recency_bias, score_weight
):
    cache_count = lax.axis_size("cache")
    place = lax.axis_index("cache")
    cand_rows, users_here, width = cand_states.shape
    head_width = in_proj.shape[2]
    heads = recency_bias.shape[0]
    events = history.shape[3]
    half_scale = 0.5 * (head_width // heads) ** (-0.5)

    swap_core, swap_chip = swap("cand", 1), swap("cand", 2)
    swap_both = swap("cand", 3)
    swap_page = swap("cache", 1)

    states = jnp.moveaxis(cand_states, 1, 0)
    in_matrix = in_proj.reshape(width, 4 * head_width)
    table = bias_rows(recency_bias, cache_count * events // BLOCK)
    first_bias = recency_bias[:, 0]

    def lookup(values, places):
        index = jnp.arange(values.shape[0], dtype=jnp.int32)
        return jnp.sum(jnp.where(places[:, None] == index, values, 0), axis=1)

    def picks_of(users, first, second, which, others):
        used = lookup(lengths, users) // BLOCK
        columns = [
            users, used, jnp.remainder(first - users, cache_count),
            jnp.remainder(second - users, cache_count), jnp.broadcast_to(which, users.shape), others,
        ]
        return jnp.stack(columns, axis=1).reshape(-1).astype(jnp.int32)

    def spread(near, far):
        return [near[0], swap_core(near[1]), swap_chip(far[0]), swap_both(far[1])]

    if cache_count == 8 and users_here == 2:
        line = [
            [0, 1, 2, 3, 3, 2, 1, 0],
            [1, 2, 3, 0, 3, 2, 0, 1],
            [2, 1, 0, 3, 0, 1, 3, 2],
            [3, 2, 1, 0, 0, 1, 2, 3],
        ]
        slots = [
            [(line[p // 2][k] * 2 + q) * 2 + k // 4 for q in (1 - p % 2, p % 2) for k in range(8)]
            for p in range(8)
        ]
        slots = lax.dynamic_index_in_dim(jnp.array(slots, jnp.int32), place, 0, False)
        users = lookup(rank_users, slots)
        at_end = (place < 2) | (place >= 6)
        exchange_outer = swap("cache", 2)
        exchange_inner = functools.partial(
            lax.ppermute, axis_name="cache", perm=[(2, 4), (4, 2), (3, 5), (5, 3)]
        )
        picks = picks_of(
            users[8:], place, place ^ 1, jnp.where(at_end, 0, 1), jnp.roll(users[:8], -2)
        )
        query_only = ((2, half_scale),)
        all_others = ((0, 1.0), (1, 1.0), (3, 1.0))

        def either(first, second):
            return jnp.where(at_end, first, second)

        def heads_of(step, queries, pages, member=0, sends=False):
            return attend(
                cache_count, picks, step, queries, history, pages, member, table, sends
            )

        mine_a, mine_b = states[0], states[1]
        across_a, near_a, near_b = swap_chip(mine_a), swap_core(mine_a), swap_core(mine_b)
        mine_b, near_a = tied(mine_b, near_a)
        across_b = swap_chip(mine_b)
        waiting, sending = pages_of(users[:2], 2, history)
        page = swap_page(waiting)
        query_near_a, query_near_b = project(
            query_only, [mine_a, near_a, mine_b, near_b], in_matrix, groups=2
        )
        across_a, query_near_a = tied(across_a, query_near_a)
        rows_a = [mine_a, near_a, across_a, swap_core(across_a)]
        query_a = project_behind(query_near_a, half_scale, rows_a[2:], in_matrix)
        query_a, sending = tied(query_a, sending)

        outer, inner, totals = [], [], []
        for step in range(8):
            if step == 0:
                to_outer, to_inner, queries = query_a, query_a, [query_a]
            if step == 1:
                to_outer, to_inner = either(query_b, inner[0]), outer[0]
                queries = [outer[0], inner[0]]
            if step == 2:
                to_outer, to_inner = either(totals[1], inner[1]), outer[1]
                queries = [outer[1], inner[1]]
            if step == 3:
                to_outer, to_inner = either(totals[2], inner[2]), query_b
                queries = [outer[2], outer[0]]
                to_outer, out_mine = tied(to_outer, out_proj)
                out_across, out_near = swap_chip(out_mine), swap_core(out_mine)
            if step == 4:
                to_outer, to_inner = either(totals[3], inner[3]), outer[3] + totals[1]
                queries = [outer[3], inner[2]]
            if step == 5:
                to_outer, to_inner = either(totals[4], query_b), outer[4] + totals[2]
                queries = [outer[4], inner[3]]
            if step == 6:
                to_outer, to_inner = either(totals[5], inner[5] + totals[3]), outer[5] + totals[4]
                queries = [outer[5], outer[1]]
            if step == 7:
                to_outer, to_inner = either(totals[6], inner[6] + totals[6]), outer[6] + totals[5]
                queries = [query_b]
            held, page = page, swap_page(sending) if step < 7 else page
            outer.append(exchange_outer(to_outer))
            inner.append(exchange_inner(to_inner))
            total, *sending = heads_of(step, [[array] for array in queries], held, 0, step < 6)
            extra = []
            if step == 0:
                pieces = [swap_core(piece) for piece in jnp.split(across_b, 2)]
                rows_b = [mine_b, near_b, across_b, *pieces]
                extra = [project_behind(query_near_b, half_scale, rows_b[2:], in_matrix)]
            if step == 1:
                rows_a[0], total = tied(rows_a[0], total)
                extra = project(all_others, rows_a, in_matrix)
            if step == 2:
                rows_b[0], total = tied(rows_b[0], total)
                extra = project(all_others, rows_b, in_matrix)
            if step == 5:
                extra = [out_mine, out_near, out_across, swap_core(out_across)]
            if step == 7:
                parts_a = [totals[0], either(outer[6], outer[2]), inner[4]]
                far_a = finish(first_bias, 1, parts_a, *heads_a)
                near_a = finish(first_bias, 0, parts_a, *heads_a)
                extra = combine(states[0], score_weight, spread(near_a, far_a), out_rows)
            if step < 3:
                page, outer[step] = tied(page, outer[step])
            outer[step], inner[step], total, *rest = tied(
                outer[step], inner[step], total, *sending, *extra
            )
            totals.append(total)
            if sending:
                sending, *extra = rest
            else:
                extra = rest
            if step == 0:
                (query_b,) = extra
            if step == 0:
                (query_b,) = extra
            if step == 1:
                heads_a = (*extra, [query_a])
            if step == 2:
                heads_b = (*extra, [query_b])
            if step == 5:
                out_rows = extra
        parts_b = [totals[7], outer[7], inner[7]]
        far_b = finish(first_bias, 1, parts_b, *heads_b)
        near_b = finish(first_bias, 0, parts_b, *heads_b)
        layer, scores = combine(
            states[1], score_weight, spread(near_b, far_b), out_rows, extra
        )
        return layer, scores.T

    chosen = jnp.take(history[0], rank_users, axis=0).reshape(
        cache_count, users_here, 2, events, head_width
    )
    arrived = lax.all_to_all(chosen, "cache", split_axis=0, concat_axis=0, tiled=True)
    out_across = swap_chip(out_proj)
    weight_rows = [out_proj, swap_core(out_proj), out_across, swap_core(out_across)]
    my_users = lax.dynamic_slice_in_dim(rank_users, place * users_here, users_here)
    layers, scores = [], []
    for member in range(users_here):
        across = swap_chip(states[member])
        rows = [states[member], swap_core(states[member]), across, swap_core(across)]
        kinds = ((0, 1.0), (1, 1.0), (2, half_scale), (3, 1.0))
        gates, values, queries, keys = project(kinds, rows, in_matrix)

        def add_pair(step, total, member=member, queries=queries):
            pair = lax.dynamic_slice(
                arrived, (2 * step, member, 0, 0, 0), (2, 1, 2, events, head_width)
            )
            user = my_users[member][None]
            picks = picks_of(user, 2 * step, 2 * step + 1, 0, user).at[0].set(0)
            (part,) = attend(cache_count, picks, 0, [[queries]], pair[:1], pair[1:, 0], 0, table)
            return total + part.astype(jnp.float32)

        total = lax.fori_loop(
            0, cache_count // 2, add_pair, jnp.zeros(queries.shape, jnp.float32)
        )
        near, far = (
            finish(first_bias, half, [total], gates, values, keys, [queries]) for half in (0, 1)
        )
        layer, score = combine(states[member], score_weight, spread(near, far), weight_rows)
        layers.append(layer)
        scores.append(score)
    return jnp.stack(layers, axis=1), jnp.concatenate(scores, axis=0).T


def solution(mesh):
    in_specs = (
        P("cand", "cache", None),
        P(None, None, "cand"),
        P("cand", None),
        P("cache", None, None, None, "cand"),
        P(),
        P(),
        P("cand", None),
        P(),
    )
    out_specs = (P("cand", "cache", None), P("cand", "cache"))
    return jax.shard_map(local, mesh=mesh, in_specs=in_specs, out_specs=out_specs, check_vma=False)
```

```python
import functools

import jax
import jax.numpy as jnp
from jax import lax
from jax.experimental import pallas as pl
from jax.experimental.pallas import tpu as pltpu
from jax.sharding import PartitionSpec as P

BLOCK = 128
EPSILON = 1e-06
MASKED = -1e30
MIB = 1024 * 1024
QUICK = pl.CostEstimate(flops=1, bytes_accessed=1, transcendentals=0)


def local_call(kernel, name, args, outs, scratch=(), places=(), held=True):
    places = dict(places)
    placed = [
        arg
        if places.get(i) == pltpu.SMEM
        else pltpu.with_memory_space_constraint(arg, places.get(i, pltpu.VMEM))
        for i, arg in enumerate(args)
    ]
    return pl.pallas_call(
        kernel,
        in_specs=[
            pl.BlockSpec(memory_space=places.get(i, pltpu.VMEM)) for i in range(len(args))
        ],
        out_specs=[pl.BlockSpec(memory_space=pltpu.VMEM)] * len(outs),
        out_shape=[
            pltpu.VMEM(shape, dtype) if held else jax.ShapeDtypeStruct(shape, dtype)
            for shape, dtype in outs
        ],
        scratch_shapes=list(scratch),
        compiler_params=pltpu.CompilerParams(vmem_limit_bytes=20 * MIB),
        cost_estimate=QUICK,
        name=name,
    )(*placed)


def tied(*arrays):
    return lax.optimization_barrier(arrays)


def bias_rows(recency_bias, most_blocks):
    bucket_count = recency_bias.shape[1]
    ends = jnp.arange(1, most_blocks + 1, dtype=jnp.int32)[:, None] * BLOCK
    distance = ends - jnp.arange(BLOCK, dtype=jnp.int32)[None, :]
    bucket = sum((distance >= 2**k).astype(jnp.int32) for k in range(bucket_count - 1))
    rows = sum(
        jnp.where(bucket[None] == b, recency_bias[:, b][:, None, None], 0.0)
        for b in range(bucket_count)
    )
    past = jnp.full((recency_bias.shape[0], 1, BLOCK), MASKED, jnp.float32)
    return jnp.concatenate([past, rows * 0.5], axis=1)


def attend_kernel(cache_count, step, member, halves, sends, picks, history, other, table, *refs):
    refs, (query, both, totals, sem, other_sem, next_sem) = refs[:-6], refs[-6:]
    queries, (out, *next_page) = (refs[:-2], refs[-2:]) if sends else (refs[:-1], refs[-1:])
    heads = table.shape[0]
    rows, width = out.shape
    size = width // heads
    blocks = both.shape[2] // BLOCK
    user, blocks_used, *shifts, which, next_user = (picks[6 * step + i] for i in range(6))
    fetch = pltpu.make_async_copy(history.at[0, user], both.at[0], sem)
    fetch.start()
    fetch_other = pltpu.make_async_copy(other.at[0], both.at[1], other_sem)
    fetch_other.start()
    if sends:
        next_fetch = pltpu.make_async_copy(history.at[0, next_user], next_page[0].at[0], next_sem)
        next_fetch.start()
    if len(queries) == halves:
        for i, ref in enumerate(queries):
            query[i * rows // halves : (i + 1) * rows // halves, :] = ref[...]
    else:
        for i, (first, second) in enumerate(zip(queries[:halves], queries[halves:])):
            query[i * rows // halves : (i + 1) * rows // halves, :] = jnp.where(
                which == 0, first[...], second[...]
            )

    chunk = min(2, blocks)
    needed = jnp.maximum(blocks_used - jnp.minimum(*shifts) + cache_count - 1, 0) // cache_count
    chunks = jnp.maximum((jnp.minimum(needed, blocks) + chunk - 1) // chunk, 1)

    def add_chunk(index, carry):
        page, first = 1 - index // chunks, index % chunks * chunk

        @pl.when(index == chunks)
        def _():
            fetch.wait()

        shift = jnp.where(page == 0, shifts[0], shifts[1])
        left = [
            jnp.maximum(blocks_used - ((first + i) * cache_count + shift), 0) for i in range(chunk)
        ]
        events = pl.ds(pl.multiple_of(first * BLOCK, BLOCK), chunk * BLOCK)
        for head in range(heads):
            columns = slice(head * size, (head + 1) * size)
            bias = jnp.concatenate([table[head, pl.ds(m, 1), :] for m in left], axis=1)
            half = bias + lax.dot_general(
                query[:, columns],
                both[page, 0, events, columns],
                (((1,), (1,)), ((), ())),
                preferred_element_type=jnp.float32,
            )
            weights = (half + half * jnp.tanh(half)).astype(jnp.bfloat16)
            totals[:, columns] += jnp.dot(
                weights, both[page, 1, events, columns], preferred_element_type=jnp.float32
            )
        return carry

    totals[...] = jnp.zeros_like(totals)
    fetch_other.wait()
    lax.fori_loop(0, 2 * chunks, add_chunk, 0)
    out[...] = totals[...].astype(jnp.bfloat16)

    if sends:
        next_fetch.wait()


def attend(cache_count, picks, step, queries, history, other, member, table, sends=False):
    halves = len(queries[0])
    queries = [piece for array in queries for piece in array]
    rows, width = halves * queries[0].shape[0], queries[0].shape[1]
    outs = [((rows, width), jnp.bfloat16), ((1,) + history.shape[2:], history.dtype)]
    return local_call(
        functools.partial(attend_kernel, cache_count, step, member, halves, sends),
        "attend",
        [picks, history, other, table, *queries],
        outs if sends else outs[:1],
        scratch=[
            pltpu.VMEM((rows, width), jnp.bfloat16),
            pltpu.VMEM((2,) + history.shape[2:], history.dtype),
            pltpu.VMEM((rows, width), jnp.float32),
            pltpu.SemaphoreType.DMA,
            pltpu.SemaphoreType.DMA,
            pltpu.SemaphoreType.DMA,
        ],
        places={0: pltpu.SMEM, 1: pltpu.HBM},
    )


def pages_kernel(users, history, *refs):
    outs, sem = refs[:-1], refs[-1]
    rows = min(2 * BLOCK, history.shape[3])
    copies = [
        pltpu.make_async_copy(
            history.at[0, users[i], kind, pl.ds(first, rows)],
            out.at[0, kind, pl.ds(first, rows)],
            sem.at[i, kind, first // rows],
        )
        for i, out in enumerate(outs)
        for kind in range(2)
        for first in range(0, history.shape[3], rows)
    ]
    for copy in copies:
        copy.start()
    for copy in copies:
        copy.wait()


def pages_of(users, count, history):
    return local_call(
        pages_kernel,
        "pages",
        [users, history],
        [((1,) + history.shape[2:], history.dtype)] * count,
        scratch=[pltpu.SemaphoreType.DMA((count, 2, max(1, history.shape[3] // (2 * BLOCK))))],
        places={0: pltpu.SMEM, 1: pltpu.HBM},
    )


def behind_kernel(scale, weight, ahead, *refs):
    *blocks, out = refs
    rows = ahead.shape[0]
    out[:rows, :] = ahead[...]
    project_kernel(
        [(2, scale)], 1, len(blocks), weight, *blocks, out.at[pl.ds(rows, rows)]
    )


def project_behind(ahead, scale, blocks, in_matrix):
    rows, width = ahead.shape
    (queries,) = local_call(
        functools.partial(behind_kernel, scale),
        "project",
        [in_matrix, ahead, *blocks],
        [((2 * rows, width), jnp.bfloat16)],
    )
    return queries


def project_kernel(kinds, groups, count, weight, *refs):
    blocks, outs = refs[:count], refs[count:]
    total, width = outs[0].shape
    first, group = 0, 0
    for block in blocks:
        rows = block.shape[0]
        state = block[...].astype(jnp.float32)
        half_norm = 0.5 * lax.rsqrt(jnp.mean(state * state, axis=-1, keepdims=True) + EPSILON)
        for (quarter, scale), out in zip(kinds, outs[group * len(kinds) :]):
            half = half_norm * jnp.dot(
                block[...],
                weight[:, quarter * width : (quarter + 1) * width],
                preferred_element_type=jnp.float32,
            )
            out[first : first + rows, :] = (
                (half + half * jnp.tanh(half)) * scale
            ).astype(jnp.bfloat16)
        first += rows
        if first == total:
            first, group = 0, group + 1


def project(kinds, blocks, in_matrix, groups=1):
    shape = (sum(block.shape[0] for block in blocks) // groups, in_matrix.shape[1] // 4)
    return local_call(
        functools.partial(project_kernel, kinds, groups, len(blocks)),
        "project",
        [in_matrix, *blocks],
        [(shape, jnp.bfloat16)] * (len(kinds) * groups),
    )


def finish_kernel(half, count, first_bias, *refs):
    parts, heads_refs, outs = refs[:count], refs[count:-2], refs[-2:]
    gates, values, keys, *queries = heads_refs
    heads = first_bias.shape[0]
    rows, width = outs[0].shape
    size = width // heads

    def load(ref, i, columns):
        first = i * rows
        if ref.shape[0] == 4 * rows:
            first = first + half * 2 * rows
        return ref[first : first + rows, columns].astype(jnp.float32)

    for i, out in enumerate(outs):
        for head in range(heads):
            columns = slice(head * size, (head + 1) * size)
            total = sum(load(part, i, columns) for part in parts)
            products = load(queries[0], i, columns) * load(keys, i, columns)
            score = jnp.sum(products, axis=-1, keepdims=True) + first_bias[head] * 0.5
            total = total + (score + score * jnp.tanh(score)) * load(values, i, columns)
            scale = lax.rsqrt(jnp.mean(total * total, axis=-1, keepdims=True) + EPSILON)
            out[:, columns] = (total * scale * load(gates, i, columns)).astype(jnp.bfloat16)


def finish(first_bias, half, parts, gates, values, keys, query):
    rows, width = gates.shape
    return local_call(
        functools.partial(finish_kernel, half, len(parts)),
        "finish",
        [first_bias, *parts, gates, values, keys, *query],
        [((rows // 4, width), jnp.bfloat16)] * 2,
        places={0: pltpu.SMEM},
    )


def combine_kernel(count, states, score_weight, *refs):
    gated, weights, rest = refs[:count], refs[count : 2 * count], refs[2 * count :]
    *before, layer, scores = rest
    total = states[...].astype(jnp.float32)
    for part, weight in zip(gated, weights):
        total = total + jnp.dot(part[...], weight[...], preferred_element_type=jnp.float32)
    column = jnp.sum(total * score_weight[...], axis=-1, keepdims=True)
    row = jnp.transpose(jnp.broadcast_to(column, (column.shape[0], 128)))[:1]
    if before:
        layer[:, 0, :] = before[0][...]
        layer[:, 1, :] = total.astype(jnp.bfloat16)
        scores[:1, :] = before[1][...]
        scores[1:, :] = row
    else:
        layer[...] = total.astype(jnp.bfloat16)
        scores[...] = row


def combine(states, score_weight, gated, weights, before=()):
    rows, width = states.shape
    layer = (rows, 2, width) if before else (rows, width)
    return local_call(
        functools.partial(combine_kernel, len(gated)),
        "combine",
        [states, score_weight[None], *gated, *weights, *before],
        [(layer, jnp.bfloat16), ((2 if before else 1, rows), jnp.float32)],
        held=False,
    )


def swap(axis, bit):
    return functools.partial(
        lax.ppermute, axis_name=axis, perm=[(i, i ^ bit) for i in range(lax.axis_size(axis))]
    )


def local(
    cand_states, in_proj, out_proj, history, lengths, rank_users, recency_bias, score_weight
):
    cache_count = lax.axis_size("cache")
    place = lax.axis_index("cache")
    cand_rows, users_here, width = cand_states.shape
    head_width = in_proj.shape[2]
    heads = recency_bias.shape[0]
    events = history.shape[3]
    half_scale = 0.5 * (head_width // heads) ** (-0.5)

    swap_core, swap_chip = swap("cand", 1), swap("cand", 2)
    swap_both = swap("cand", 3)
    swap_page = swap("cache", 1)

    states = jnp.moveaxis(cand_states, 1, 0)
    in_matrix = in_proj.reshape(width, 4 * head_width)
    table = bias_rows(recency_bias, cache_count * events // BLOCK)
    first_bias = recency_bias[:, 0]

    def lookup(values, places):
        index = jnp.arange(values.shape[0], dtype=jnp.int32)
        return jnp.sum(jnp.where(places[:, None] == index, values, 0), axis=1)

    def picks_of(users, first, second, which, others):
        used = lookup(lengths, users) // BLOCK
        columns = [
            users, used, jnp.remainder(first - users, cache_count),
            jnp.remainder(second - users, cache_count), jnp.broadcast_to(which, users.shape), others,
        ]
        return jnp.stack(columns, axis=1).reshape(-1).astype(jnp.int32)

    def spread(near, far):
        return [near[0], swap_core(near[1]), swap_chip(far[0]), swap_both(far[1])]

    if cache_count == 8 and users_here == 2:
        line = [
            [0, 1, 2, 3, 3, 2, 1, 0],
            [1, 2, 3, 0, 3, 2, 0, 1],
            [2, 1, 0, 3, 0, 1, 3, 2],
            [3, 2, 1, 0, 0, 1, 2, 3],
        ]
        slots = [
            [(line[p // 2][k] * 2 + q) * 2 + k // 4 for q in (1 - p % 2, p % 2) for k in range(8)]
            for p in range(8)
        ]
        slots = lax.dynamic_index_in_dim(jnp.array(slots, jnp.int32), place, 0, False)
        users = lookup(rank_users, slots)
        at_end = (place < 2) | (place >= 6)
        exchange_outer = swap("cache", 2)
        exchange_inner = functools.partial(
            lax.ppermute, axis_name="cache", perm=[(2, 4), (4, 2), (3, 5), (5, 3)]
        )
        picks = picks_of(
            users[8:], place, place ^ 1, jnp.where(at_end, 0, 1), jnp.roll(users[:8], -2)
        )
        query_only = ((2, half_scale),)
        all_others = ((0, 1.0), (1, 1.0), (3, 1.0))

        def either(first, second):
            return jnp.where(at_end, first, second)

        def heads_of(step, queries, pages, member=0, sends=False):
            return attend(
                cache_count, picks, step, queries, history, pages, member, table, sends
            )

        mine_a, mine_b = states[0], states[1]
        across_a, near_a, near_b = swap_chip(mine_a), swap_core(mine_a), swap_core(mine_b)
        mine_b, near_a = tied(mine_b, near_a)
        across_b = swap_chip(mine_b)
        waiting, sending = pages_of(users[:2], 2, history)
        page = swap_page(waiting)
        query_near_a, query_near_b = project(
            query_only, [mine_a, near_a, mine_b, near_b], in_matrix, groups=2
        )
        across_a, query_near_a = tied(across_a, query_near_a)
        rows_a = [mine_a, near_a, across_a, swap_core(across_a)]
        query_a = project_behind(query_near_a, half_scale, rows_a[2:], in_matrix)
        query_a, sending = tied(query_a, sending)

        outer, inner, totals = [], [], []
        for step in range(8):
            if step == 0:
                to_outer, to_inner, queries = query_a, query_a, [query_a]
            if step == 1:
                to_outer, to_inner = either(query_b, inner[0]), outer[0]
                queries = [outer[0], inner[0]]
            if step == 2:
                to_outer, to_inner = either(totals[1], inner[1]), outer[1]
                queries = [outer[1], inner[1]]
            if step == 3:
                to_outer, to_inner = either(totals[2], inner[2]), query_b
                queries = [outer[2], outer[0]]
                to_outer, out_mine = tied(to_outer, out_proj)
                out_across, out_near = swap_chip(out_mine), swap_core(out_mine)
            if step == 4:
                to_outer, to_inner = either(totals[3], inner[3]), outer[3] + totals[1]
                queries = [outer[3], inner[2]]
            if step == 5:
                to_outer, to_inner = either(totals[4], query_b), outer[4] + totals[2]
                queries = [outer[4], inner[3]]
            if step == 6:
                to_outer, to_inner = either(totals[5], inner[5] + totals[3]), outer[5] + totals[4]
                queries = [outer[5], outer[1]]
            if step == 7:
                to_outer, to_inner = either(totals[6], inner[6] + totals[6]), outer[6] + totals[5]
                queries = [query_b]
            held, page = page, swap_page(sending) if step < 7 else page
            outer.append(exchange_outer(to_outer))
            inner.append(exchange_inner(to_inner))
            total, *sending = heads_of(step, [[array] for array in queries], held, 0, step < 6)
            extra = []
            if step == 0:
                pieces = [swap_core(piece) for piece in jnp.split(across_b, 2)]
                rows_b = [mine_b, near_b, across_b, *pieces]
                extra = [project_behind(query_near_b, half_scale, rows_b[2:], in_matrix)]
            if step == 1:
                rows_a[0], total = tied(rows_a[0], total)
                extra = project(all_others, rows_a, in_matrix)
            if step == 2:
                rows_b[0], total = tied(rows_b[0], total)
                extra = project(all_others, rows_b, in_matrix)
            if step == 5:
                extra = [out_mine, out_near, out_across, swap_core(out_across)]
            if step == 7:
                parts_a = [totals[0], either(outer[6], outer[2]), inner[4]]
                far_a = finish(first_bias, 1, parts_a, *heads_a)
                near_a = finish(first_bias, 0, parts_a, *heads_a)
                extra = combine(states[0], score_weight, spread(near_a, far_a), out_rows)
            if step < 3:
                page, outer[step] = tied(page, outer[step])
            outer[step], inner[step], total, *rest = tied(
                outer[step], inner[step], total, *sending, *extra
            )
            totals.append(total)
            if sending:
                sending, *extra = rest
            else:
                extra = rest
            if step == 0:
                (query_b,) = extra
            if step == 0:
                (query_b,) = extra
            if step == 1:
                heads_a = (*extra, [query_a])
            if step == 2:
                heads_b = (*extra, [query_b])
            if step == 5:
                out_rows = extra
        parts_b = [totals[7], outer[7], inner[7]]
        far_b = finish(first_bias, 1, parts_b, *heads_b)
        near_b = finish(first_bias, 0, parts_b, *heads_b)
        layer, scores = combine(
            states[1], score_weight, spread(near_b, far_b), out_rows, extra
        )
        return layer, scores.T

    chosen = jnp.take(history[0], rank_users, axis=0).reshape(
        cache_count, users_here, 2, events, head_width
    )
    arrived = lax.all_to_all(chosen, "cache", split_axis=0, concat_axis=0, tiled=True)
    out_across = swap_chip(out_proj)
    weight_rows = [out_proj, swap_core(out_proj), out_across, swap_core(out_across)]
    my_users = lax.dynamic_slice_in_dim(rank_users, place * users_here, users_here)
    layers, scores = [], []
    for member in range(users_here):
        across = swap_chip(states[member])
        rows = [states[member], swap_core(states[member]), across, swap_core(across)]
        kinds = ((0, 1.0), (1, 1.0), (2, half_scale), (3, 1.0))
        gates, values, queries, keys = project(kinds, rows, in_matrix)

        def add_pair(step, total, member=member, queries=queries):
            pair = lax.dynamic_slice(
                arrived, (2 * step, member, 0, 0, 0), (2, 1, 2, events, head_width)
            )
            user = my_users[member][None]
            picks = picks_of(user, 2 * step, 2 * step + 1, 0, user).at[0].set(0)
            (part,) = attend(cache_count, picks, 0, [[queries]], pair[:1], pair[1:, 0], 0, table)
            return total + part.astype(jnp.float32)

        total = lax.fori_loop(
            0, cache_count // 2, add_pair, jnp.zeros(queries.shape, jnp.float32)
        )
        near, far = (
            finish(first_bias, half, [total], gates, values, keys, [queries]) for half in (0, 1)
        )
        layer, score = combine(states[member], score_weight, spread(near, far), weight_rows)
        layers.append(layer)
        scores.append(score)
    return jnp.stack(layers, axis=1), jnp.concatenate(scores, axis=0).T


def solution(mesh):
    in_specs = (
        P("cand", "cache", None),
        P(None, None, "cand"),
        P("cand", None),
        P("cache", None, None, None, "cand"),
        P(),
        P(),
        P("cand", None),
        P(),
    )
    out_specs = (P("cand", "cache", None), P("cand", "cache"))
    return jax.shard_map(local, mesh=mesh, in_specs=in_specs, out_specs=out_specs, check_vma=False)
```

```python
import functools

import jax
import jax.numpy as jnp
from jax import lax
from jax.experimental import pallas as pl
from jax.experimental.pallas import tpu as pltpu
from jax.sharding import PartitionSpec as P

BLOCK = 128
EPSILON = 1e-06
MASKED = -1e30
MIB = 1024 * 1024
QUICK = pl.CostEstimate(flops=1, bytes_accessed=1, transcendentals=0)


def local_call(kernel, name, args, outs, scratch=(), places=(), held=True):
    places = dict(places)
    placed = [
        arg
        if places.get(i) == pltpu.SMEM
        else pltpu.with_memory_space_constraint(arg, places.get(i, pltpu.VMEM))
        for i, arg in enumerate(args)
    ]
    return pl.pallas_call(
        kernel,
        in_specs=[
            pl.BlockSpec(memory_space=places.get(i, pltpu.VMEM)) for i in range(len(args))
        ],
        out_specs=[pl.BlockSpec(memory_space=pltpu.VMEM)] * len(outs),
        out_shape=[
            pltpu.VMEM(shape, dtype) if held else jax.ShapeDtypeStruct(shape, dtype)
            for shape, dtype in outs
        ],
        scratch_shapes=list(scratch),
        compiler_params=pltpu.CompilerParams(vmem_limit_bytes=20 * MIB),
        cost_estimate=QUICK,
        name=name,
    )(*placed)


def tied(*arrays):
    return lax.optimization_barrier(arrays)


def bias_rows(recency_bias, most_blocks):
    bucket_count = recency_bias.shape[1]
    ends = jnp.arange(1, most_blocks + 1, dtype=jnp.int32)[:, None] * BLOCK
    distance = ends - jnp.arange(BLOCK, dtype=jnp.int32)[None, :]
    bucket = sum((distance >= 2**k).astype(jnp.int32) for k in range(bucket_count - 1))
    rows = sum(
        jnp.where(bucket[None] == b, recency_bias[:, b][:, None, None], 0.0)
        for b in range(bucket_count)
    )
    past = jnp.full((recency_bias.shape[0], 1, BLOCK), MASKED, jnp.float32)
    return jnp.concatenate([past, rows * 0.5], axis=1)


def attend_kernel(cache_count, step, member, halves, sends, picks, history, other, table, *refs):
    refs, (query, both, totals, sem, other_sem, next_sem) = refs[:-6], refs[-6:]
    queries, (out, *next_page) = (refs[:-2], refs[-2:]) if sends else (refs[:-1], refs[-1:])
    heads = table.shape[0]
    rows, width = out.shape
    size = width // heads
    blocks = both.shape[2] // BLOCK
    user, blocks_used, *shifts, which, next_user = (picks[6 * step + i] for i in range(6))
    fetch = pltpu.make_async_copy(history.at[0, user], both.at[0], sem)
    fetch.start()
    fetch_other = pltpu.make_async_copy(other.at[0], both.at[1], other_sem)
    fetch_other.start()
    if sends:
        next_fetch = pltpu.make_async_copy(history.at[0, next_user], next_page[0].at[0], next_sem)
        next_fetch.start()
    if len(queries) == halves:
        for i, ref in enumerate(queries):
            query[i * rows // halves : (i + 1) * rows // halves, :] = ref[...]
    else:
        for i, (first, second) in enumerate(zip(queries[:halves], queries[halves:])):
            query[i * rows // halves : (i + 1) * rows // halves, :] = jnp.where(
                which == 0, first[...], second[...]
            )

    chunk = min(2, blocks)
    needed = jnp.maximum(blocks_used - jnp.minimum(*shifts) + cache_count - 1, 0) // cache_count
    chunks = jnp.maximum((jnp.minimum(needed, blocks) + chunk - 1) // chunk, 1)

    def add_chunk(index, carry):
        page, first = 1 - index // chunks, index % chunks * chunk

        @pl.when(index == chunks)
        def _():
            fetch.wait()

        shift = jnp.where(page == 0, shifts[0], shifts[1])
        left = [
            jnp.maximum(blocks_used - ((first + i) * cache_count + shift), 0) for i in range(chunk)
        ]
        events = pl.ds(pl.multiple_of(first * BLOCK, BLOCK), chunk * BLOCK)
        for head in range(heads):
            columns = slice(head * size, (head + 1) * size)
            bias = jnp.concatenate([table[head, pl.ds(m, 1), :] for m in left], axis=1)
            half = bias + lax.dot_general(
                query[:, columns],
                both[page, 0, events, columns],
                (((1,), (1,)), ((), ())),
                preferred_element_type=jnp.float32,
            )
            weights = (half + half * jnp.tanh(half)).astype(jnp.bfloat16)
            totals[:, columns] += jnp.dot(
                weights, both[page, 1, events, columns], preferred_element_type=jnp.float32
            )
        return carry

    totals[...] = jnp.zeros_like(totals)
    fetch_other.wait()
    lax.fori_loop(0, 2 * chunks, add_chunk, 0)
    out[...] = totals[...].astype(jnp.bfloat16)

    if sends:
        next_fetch.wait()


def attend(cache_count, picks, step, queries, history, other, member, table, sends=False):
    halves = len(queries[0])
    queries = [piece for array in queries for piece in array]
    rows, width = halves * queries[0].shape[0], queries[0].shape[1]
    outs = [((rows, width), jnp.bfloat16), ((1,) + history.shape[2:], history.dtype)]
    return local_call(
        functools.partial(attend_kernel, cache_count, step, member, halves, sends),
        "attend",
        [picks, history, other, table, *queries],
        outs if sends else outs[:1],
        scratch=[
            pltpu.VMEM((rows, width), jnp.bfloat16),
            pltpu.VMEM((2,) + history.shape[2:], history.dtype),
            pltpu.VMEM((rows, width), jnp.float32),
            pltpu.SemaphoreType.DMA,
            pltpu.SemaphoreType.DMA,
            pltpu.SemaphoreType.DMA,
        ],
        places={0: pltpu.SMEM, 1: pltpu.HBM},
    )


def pages_kernel(users, history, *refs):
    outs, sem = refs[:-1], refs[-1]
    rows = min(2 * BLOCK, history.shape[3])
    copies = [
        pltpu.make_async_copy(
            history.at[0, users[i], kind, pl.ds(first, rows)],
            out.at[0, kind, pl.ds(first, rows)],
            sem.at[i, kind, first // rows],
        )
        for i, out in enumerate(outs)
        for kind in range(2)
        for first in range(0, history.shape[3], rows)
    ]
    for copy in copies:
        copy.start()
    for copy in copies:
        copy.wait()


def pages_of(users, count, history):
    return local_call(
        pages_kernel,
        "pages",
        [users, history],
        [((1,) + history.shape[2:], history.dtype)] * count,
        scratch=[pltpu.SemaphoreType.DMA((count, 2, max(1, history.shape[3] // (2 * BLOCK))))],
        places={0: pltpu.SMEM, 1: pltpu.HBM},
    )


def behind_kernel(scale, weight, ahead, *refs):
    *blocks, out = refs
    rows = ahead.shape[0]
    out[:rows, :] = ahead[...]
    project_kernel(
        [(2, scale)], 1, len(blocks), weight, *blocks, out.at[pl.ds(rows, rows)]
    )


def project_behind(ahead, scale, blocks, in_matrix):
    rows, width = ahead.shape
    (queries,) = local_call(
        functools.partial(behind_kernel, scale),
        "project",
        [in_matrix, ahead, *blocks],
        [((2 * rows, width), jnp.bfloat16)],
    )
    return queries


def project_kernel(kinds, groups, count, weight, *refs):
    blocks, outs = refs[:count], refs[count:]
    total, width = outs[0].shape
    first, group = 0, 0
    for block in blocks:
        rows = block.shape[0]
        state = block[...].astype(jnp.float32)
        half_norm = 0.5 * lax.rsqrt(jnp.mean(state * state, axis=-1, keepdims=True) + EPSILON)
        for (quarter, scale), out in zip(kinds, outs[group * len(kinds) :]):
            half = half_norm * jnp.dot(
                block[...],
                weight[:, quarter * width : (quarter + 1) * width],
                preferred_element_type=jnp.float32,
            )
            out[first : first + rows, :] = (
                (half + half * jnp.tanh(half)) * scale
            ).astype(jnp.bfloat16)
        first += rows
        if first == total:
            first, group = 0, group + 1


def project(kinds, blocks, in_matrix, groups=1):
    shape = (sum(block.shape[0] for block in blocks) // groups, in_matrix.shape[1] // 4)
    return local_call(
        functools.partial(project_kernel, kinds, groups, len(blocks)),
        "project",
        [in_matrix, *blocks],
        [(shape, jnp.bfloat16)] * (len(kinds) * groups),
    )


def finish_kernel(half, count, first_bias, *refs):
    parts, heads_refs, outs = refs[:count], refs[count:-2], refs[-2:]
    gates, values, keys, *queries = heads_refs
    heads = first_bias.shape[0]
    rows, width = outs[0].shape
    size = width // heads

    def load(ref, i, columns):
        first = i * rows
        if ref.shape[0] == 4 * rows:
            first = first + half * 2 * rows
        return ref[first : first + rows, columns].astype(jnp.float32)

    for i, out in enumerate(outs):
        for head in range(heads):
            columns = slice(head * size, (head + 1) * size)
            total = sum(load(part, i, columns) for part in parts)
            products = load(queries[0], i, columns) * load(keys, i, columns)
            score = jnp.sum(products, axis=-1, keepdims=True) + first_bias[head] * 0.5
            total = total + (score + score * jnp.tanh(score)) * load(values, i, columns)
            scale = lax.rsqrt(jnp.mean(total * total, axis=-1, keepdims=True) + EPSILON)
            out[:, columns] = (total * scale * load(gates, i, columns)).astype(jnp.bfloat16)


def finish(first_bias, half, parts, gates, values, keys, query):
    rows, width = gates.shape
    return local_call(
        functools.partial(finish_kernel, half, len(parts)),
        "finish",
        [first_bias, *parts, gates, values, keys, *query],
        [((rows // 4, width), jnp.bfloat16)] * 2,
        places={0: pltpu.SMEM},
    )


def combine_kernel(count, states, score_weight, *refs):
    gated, weights, rest = refs[:count], refs[count : 2 * count], refs[2 * count :]
    *before, layer, scores = rest
    total = states[...].astype(jnp.float32)
    for part, weight in zip(gated, weights):
        total = total + jnp.dot(part[...], weight[...], preferred_element_type=jnp.float32)
    column = jnp.sum(total * score_weight[...], axis=-1, keepdims=True)
    row = jnp.transpose(jnp.broadcast_to(column, (column.shape[0], 128)))[:1]
    if before:
        layer[:, 0, :] = before[0][...]
        layer[:, 1, :] = total.astype(jnp.bfloat16)
        scores[:1, :] = before[1][...]
        scores[1:, :] = row
    else:
        layer[...] = total.astype(jnp.bfloat16)
        scores[...] = row


def combine(states, score_weight, gated, weights, before=()):
    rows, width = states.shape
    layer = (rows, 2, width) if before else (rows, width)
    return local_call(
        functools.partial(combine_kernel, len(gated)),
        "combine",
        [states, score_weight[None], *gated, *weights, *before],
        [(layer, jnp.bfloat16), ((2 if before else 1, rows), jnp.float32)],
        held=False,
    )


def swap(axis, bit):
    return functools.partial(
        lax.ppermute, axis_name=axis, perm=[(i, i ^ bit) for i in range(lax.axis_size(axis))]
    )


def local(
    cand_states, in_proj, out_proj, history, lengths, rank_users, recency_bias, score_weight
):
    cache_count = lax.axis_size("cache")
    place = lax.axis_index("cache")
    cand_rows, users_here, width = cand_states.shape
    head_width = in_proj.shape[2]
    heads = recency_bias.shape[0]
    events = history.shape[3]
    half_scale = 0.5 * (head_width // heads) ** (-0.5)

    swap_core, swap_chip = swap("cand", 1), swap("cand", 2)
    swap_both = swap("cand", 3)
    swap_page = swap("cache", 1)

    states = [cand_states[:, member] for member in range(users_here)]
    in_matrix = in_proj.reshape(width, 4 * head_width)
    table = bias_rows(recency_bias, cache_count * events // BLOCK)
    first_bias = recency_bias[:, 0]

    def lookup(values, places):
        index = jnp.arange(values.shape[0], dtype=jnp.int32)
        return jnp.sum(jnp.where(places[:, None] == index, values, 0), axis=1)

    def picks_of(users, first, second, which, others):
        used = lookup(lengths, users) // BLOCK
        columns = [
            users, used, jnp.remainder(first - users, cache_count),
            jnp.remainder(second - users, cache_count), jnp.broadcast_to(which, users.shape), others,
        ]
        return jnp.stack(columns, axis=1).reshape(-1).astype(jnp.int32)

    def spread(near, far):
        return [near[0], swap_core(near[1]), swap_chip(far[0]), swap_both(far[1])]

    if cache_count == 8 and users_here == 2:
        line = [
            [0, 1, 2, 3, 3, 2, 1, 0],
            [1, 2, 3, 0, 3, 2, 0, 1],
            [2, 1, 0, 3, 0, 1, 3, 2],
            [3, 2, 1, 0, 0, 1, 2, 3],
        ]
        slots = [
            [(line[p // 2][k] * 2 + q) * 2 + k // 4 for q in (1 - p % 2, p % 2) for k in range(8)]
            for p in range(8)
        ]
        slots = lax.dynamic_index_in_dim(jnp.array(slots, jnp.int32), place, 0, False)
        users = lookup(rank_users, slots)
        at_end = (place < 2) | (place >= 6)
        exchange_outer = swap("cache", 2)
        exchange_inner = functools.partial(
            lax.ppermute, axis_name="cache", perm=[(2, 4), (4, 2), (3, 5), (5, 3)]
        )
        picks = picks_of(
            users[8:], place, place ^ 1, jnp.where(at_end, 0, 1), jnp.roll(users[:8], -2)
        )
        query_only = ((2, half_scale),)
        all_others = ((0, 1.0), (1, 1.0), (3, 1.0))

        def either(first, second):
            return jnp.where(at_end, first, second)

        def heads_of(step, queries, pages, member=0, sends=False):
            return attend(
                cache_count, picks, step, queries, history, pages, member, table, sends
            )

        mine_a, mine_b = states[0], states[1]
        across_a, near_a, near_b = swap_chip(mine_a), swap_core(mine_a), swap_core(mine_b)
        mine_b, near_a = tied(mine_b, near_a)
        across_b = swap_chip(mine_b)
        waiting, sending = pages_of(users[:2], 2, history)
        page = swap_page(waiting)
        query_near_a, query_near_b = project(
            query_only, [mine_a, near_a, mine_b, near_b], in_matrix, groups=2
        )
        across_a, query_near_a = tied(across_a, query_near_a)
        rows_a = [mine_a, near_a, across_a, swap_core(across_a)]
        query_a = project_behind(query_near_a, half_scale, rows_a[2:], in_matrix)
        query_a, sending = tied(query_a, sending)

        outer, inner, totals = [], [], []
        for step in range(8):
            if step == 0:
                to_outer, to_inner, queries = query_a, query_a, [query_a]
            if step == 1:
                to_outer, to_inner = either(query_b, inner[0]), outer[0]
                queries = [outer[0], inner[0]]
            if step == 2:
                to_outer, to_inner = either(totals[1], inner[1]), outer[1]
                queries = [outer[1], inner[1]]
            if step == 3:
                to_outer, to_inner = either(totals[2], inner[2]), query_b
                queries = [outer[2], outer[0]]
                to_outer, to_inner, out_mine = tied(to_outer, to_inner, out_proj)
                out_across, out_near = swap_chip(out_mine), swap_core(out_mine)
            if step == 4:
                to_outer, to_inner = either(totals[3], inner[3]), outer[3] + totals[1]
                queries = [outer[3], inner[2]]
            if step == 5:
                to_outer, to_inner = either(totals[4], query_b), outer[4] + totals[2]
                queries = [outer[4], inner[3]]
            if step == 6:
                to_outer, to_inner = either(totals[5], inner[5] + totals[3]), outer[5] + totals[4]
                queries = [outer[5], outer[1]]
            if step == 7:
                to_outer, to_inner = either(totals[6], inner[6] + totals[6]), outer[6] + totals[5]
                queries = [query_b]
            held, page = page, swap_page(sending) if step < 7 else page
            outer.append(exchange_outer(to_outer))
            inner.append(exchange_inner(to_inner))
            total, *sending = heads_of(step, [[array] for array in queries], held, 0, step < 6)
            extra = []
            if step == 0:
                pieces = [swap_core(piece) for piece in jnp.split(across_b, 2)]
                rows_b = [mine_b, near_b, across_b, *pieces]
                extra = [project_behind(query_near_b, half_scale, rows_b[2:], in_matrix)]
            if step == 1:
                rows_a[0], total = tied(rows_a[0], total)
                extra = project(all_others, rows_a, in_matrix)
            if step == 2:
                rows_b[0], total = tied(rows_b[0], total)
                extra = project(all_others, rows_b, in_matrix)
            if step == 5:
                extra = [out_mine, out_near, out_across, swap_core(out_across)]
            if step == 7:
                parts_a = [totals[0], either(outer[6], outer[2]), inner[4]]
                far_a = finish(first_bias, 1, parts_a, *heads_a)
                near_a = finish(first_bias, 0, parts_a, *heads_a)
                extra = combine(states[0], score_weight, spread(near_a, far_a), out_rows)
            if step < 3:
                page, outer[step] = tied(page, outer[step])
            outer[step], inner[step], total, *rest = tied(
                outer[step], inner[step], total, *sending, *extra
            )
            totals.append(total)
            if sending:
                sending, *extra = rest
            else:
                extra = rest
            if step == 0:
                (query_b,) = extra
            if step == 0:
                (query_b,) = extra
            if step == 1:
                heads_a = (*extra, [query_a])
            if step == 2:
                heads_b = (*extra, [query_b])
            if step == 5:
                out_rows = extra
        parts_b = [totals[7], outer[7], inner[7]]
        far_b = finish(first_bias, 1, parts_b, *heads_b)
        near_b = finish(first_bias, 0, parts_b, *heads_b)
        layer, scores = combine(
            states[1], score_weight, spread(near_b, far_b), out_rows, extra
        )
        return layer, scores.T

    chosen = jnp.take(history[0], rank_users, axis=0).reshape(
        cache_count, users_here, 2, events, head_width
    )
    arrived = lax.all_to_all(chosen, "cache", split_axis=0, concat_axis=0, tiled=True)
    out_across = swap_chip(out_proj)
    weight_rows = [out_proj, swap_core(out_proj), out_across, swap_core(out_across)]
    my_users = lax.dynamic_slice_in_dim(rank_users, place * users_here, users_here)
    layers, scores = [], []
    for member in range(users_here):
        across = swap_chip(states[member])
        rows = [states[member], swap_core(states[member]), across, swap_core(across)]
        kinds = ((0, 1.0), (1, 1.0), (2, half_scale), (3, 1.0))
        gates, values, queries, keys = project(kinds, rows, in_matrix)

        def add_pair(step, total, member=member, queries=queries):
            pair = lax.dynamic_slice(
                arrived, (2 * step, member, 0, 0, 0), (2, 1, 2, events, head_width)
            )
            user = my_users[member][None]
            picks = picks_of(user, 2 * step, 2 * step + 1, 0, user).at[0].set(0)
            (part,) = attend(cache_count, picks, 0, [[queries]], pair[:1], pair[1:, 0], 0, table)
            return total + part.astype(jnp.float32)

        total = lax.fori_loop(
            0, cache_count // 2, add_pair, jnp.zeros(queries.shape, jnp.float32)
        )
        near, far = (
            finish(first_bias, half, [total], gates, values, keys, [queries]) for half in (0, 1)
        )
        layer, score = combine(states[member], score_weight, spread(near, far), weight_rows)
        layers.append(layer)
        scores.append(score)
    return jnp.stack(layers, axis=1), jnp.concatenate(scores, axis=0).T


def solution(mesh):
    in_specs = (
        P("cand", "cache", None),
        P(None, None, "cand"),
        P("cand", None),
        P("cache", None, None, None, "cand"),
        P(),
        P(),
        P("cand", None),
        P(),
    )
    out_specs = (P("cand", "cache", None), P("cand", "cache"))
    return jax.shard_map(local, mesh=mesh, in_specs=in_specs, out_specs=out_specs, check_vma=False)
```
